32 devices in a mesh: dp: 16 (over z, x, core), tensor: 2 (over y).
Axes of the slice: x: 2, y: 2, z: 4, core: 2. Of those that a mesh axis runs over, the one named last changes fastest.
Arguments:
- tokens: bfloat16 [8192, 1024], P(('dp', 'tensor')), may hold values from -6 to 6
- w_qkv: bfloat16 [1024, 3, 1024], P(None, None, 'tensor'), may hold values from -0.1875 to 0.1875
- b_query: float32 [1024], P('tensor'), may hold values from -3 to 3
- b_value: float32 [1024], P('tensor'), may hold values from -3 to 3
- w_out: bfloat16 [1024, 1024], P('tensor'), may hold values from -1.5 to 1.5
- b_out: float32 [1024], replicated, may hold values from -3 to 3
- gain_one: float32 [1024], replicated, may hold values from 0.25 to 1.75
- shift_one: float32 [1024], replicated, may hold values from -3 to 3
- w_up: bfloat16 [1024, 4096], P(None, 'tensor'), may hold values from -0.1875 to 0.1875
- b_up: float32 [4096], P('tensor'), may hold values from -3 to 3
- w_down: bfloat16 [4096, 1024], P('tensor'), may hold values from -0.09375 to 0.09375
- b_down: float32 [1024], replicated, may hold values from -3 to 3
- gain_two: float32 [1024], replicated, may hold values from 0.25 to 1.75
- shift_two: float32 [1024], replicated, may hold values from -3 to 3
- out_grad: bfloat16 [8192, 1024], P(('dp', 'tensor')), may hold values from -6 to 6
Outputs:
- layer_out: bfloat16 [8192, 1024], P(('dp', 'tensor'))
- grad_tokens: float32 [8192, 1024], P(('dp', 'tensor'))
- grad_w_qkv: float32 [1024, 3, 1024], P(None, None, 'tensor')
- grad_b_query: float32 [1024], P('tensor')
- grad_b_value: float32 [1024], P('tensor')
- grad_w_out: float32 [1024, 1024], P('tensor')
- grad_b_out: float32 [1024], replicated
- grad_gain_one: float32 [1024], replicated
- grad_shift_one: float32 [1024], replicated
- grad_w_up: float32 [1024, 4096], P(None, 'tensor')
- grad_b_up: float32 [4096], P('tensor')
- grad_w_down: float32 [4096, 1024], P('tensor')
- grad_b_down: float32 [1024], replicated
- grad_gain_two: float32 [1024], replicated
- grad_shift_two: float32 [1024], replicated
The draws below stay inside these ranges and needn't reach their ends.
All inputs are finite; a program needn't handle non-finite values.
Results may differ from the reference program's by a relative error of at most 0.02.
Values may be sent and summed in bfloat16 or wider, within the bound.
No kernel may reach another device: no remote copies, remote signals or barrier semaphores. Data moves between devices by JAX's collectives and lax.ppermute only.
A program may use at most 128 MiB of HBM per device.

```python
import jax
import jax.numpy as jnp
from jax import lax

HEADS = 16
HEAD_DIM = 64
D = 1024
FF = 4096
LEN = 512
TOKENS = 8192
N_DP = 16


def level_of(stream_key, extent, shards, least, largest):
    def one(position, blocks):
        steps = jax.random.uniform(jax.random.fold_in(jax.random.fold_in(stream_key, 6), position), (blocks,), jnp.float32, least / len(shards), largest / len(shards))
        return jnp.repeat(jnp.exp(steps), extent[position] // blocks).reshape((-1,) + (1,) * (len(extent) - position - 1))

    level = one(*shards[0])
    for cut in shards[1:]:
        level = level * one(*cut)
    return level


def bell_draw(stream_key, shape, scale, limit, shards=(), held_as=jnp.bfloat16):
    level = level_of(stream_key, shape, shards, -0.22, 0.18) if shards else 1.0
    entries = jax.random.normal(stream_key, shape, jnp.float32) * scale * level
    return jnp.minimum(jnp.maximum(entries, -limit), limit).astype(held_as)


def setup_inputs(seed: int = 0) -> dict:
    seeds = jax.random.split(jax.random.key(seed), 16)
    return {
        "tokens": bell_draw(seeds[0], (TOKENS, D), 1.0, 6.0, ((0, 32),)),
        "w_qkv": bell_draw(seeds[1], (D, 3, D), D ** -0.5, 0.1875, ((2, 2),)),
        "b_query": bell_draw(seeds[2], (D,), 0.5, 3.0, ((0, 2),), jnp.float32),
        "b_value": bell_draw(seeds[3], (D,), 0.5, 3.0, ((0, 2),), jnp.float32),
        "w_out": bell_draw(seeds[4], (D, D), (D // 64) ** -0.5, 1.5, ((0, 2),)),
        "b_out": bell_draw(seeds[5], (D,), 0.5, 3.0, (), jnp.float32),
        "gain_one": jnp.clip(1.0 + 0.15 * jax.random.normal(seeds[6], (D,), jnp.float32), 0.25, 1.75),
        "shift_one": bell_draw(seeds[7], (D,), 0.5, 3.0, (), jnp.float32),
        "w_up": bell_draw(seeds[8], (D, FF), D ** -0.5, 0.1875, ((1, 2),)),
        "b_up": bell_draw(seeds[9], (FF,), 0.5, 3.0, ((0, 2),), jnp.float32),
        "w_down": bell_draw(seeds[10], (FF, D), FF ** -0.5, 0.09375, ((0, 2),)),
        "b_down": bell_draw(seeds[11], (D,), 0.5, 3.0, (), jnp.float32),
        "gain_two": jnp.clip(1.0 + 0.15 * jax.random.normal(seeds[12], (D,), jnp.float32), 0.25, 1.75),
        "shift_two": bell_draw(seeds[13], (D,), 0.5, 3.0, (), jnp.float32),
        "out_grad": bell_draw(seeds[14], (TOKENS, D), 1.0, 6.0, ((0, 32),)),
    }


EPSILON = 1e-12
highest = lax.Precision.HIGHEST

@jax.custom_vjp
def low(v):
    return lax.optimization_barrier(v.astype(jnp.bfloat16)).astype(jnp.float32)

@jax.custom_vjp
def low_back(v):
    return v

def low_keep(v):
    return (low(v), None)

def low_pass(kept, grad):
    return (grad,)

def back_keep(v):
    return (v, None)

def back_low(kept, grad):
    return (low(grad),)
low.defvjp(low_keep, low_pass)
low_back.defvjp(back_keep, back_low)

def norm_rows(resid, gain, shift):
    center = lax.optimization_barrier(jnp.mean(resid, axis=-1, keepdims=True))
    centred = resid - center
    variance = lax.optimization_barrier(jnp.mean(centred * centred, axis=-1, keepdims=True))
    return centred * lax.rsqrt(variance + EPSILON) * gain + shift

def block_forward(block_in, w_qkv, b_query, b_value, w_out, b_out, gain_one, shift_one, w_up, b_up, w_down, b_down, gain_two, shift_two):
    row_total = block_in.shape[0]
    seq_count = row_total // LEN
    projected = low_back(jnp.dot(block_in, w_qkv.reshape(D, 3 * D), precision=highest))
    projected = projected.reshape(row_total, 3, HEADS, HEAD_DIM)
    queries = low(projected[:, 0] + b_query.reshape(HEADS, HEAD_DIM))
    key_rows = low(projected[:, 1])
    values = low(projected[:, 2] + b_value.reshape(HEADS, HEAD_DIM))
    queries = queries.reshape(seq_count, LEN, HEADS, HEAD_DIM)
    key_rows = key_rows.reshape(seq_count, LEN, HEADS, HEAD_DIM)
    values = values.reshape(seq_count, LEN, HEADS, HEAD_DIM)
    scores = low_back(jnp.einsum('sqhd,skhd->shqk', queries, key_rows, precision=highest) * HEAD_DIM ** (-0.5))
    weights_p = low(jax.nn.softmax(scores, axis=-1))
    context = low(low_back(jnp.einsum('shqk,skhd->sqhd', weights_p, values, precision=highest)))
    context = context.reshape(row_total, D)
    attended = low_back(jnp.dot(context, w_out, precision=highest))
    hidden = norm_rows(attended + b_out + block_in, gain_one, shift_one)
    hidden_low = low(hidden)
    upward = low_back(jnp.dot(hidden_low, w_up, precision=highest)) + b_up
    active = low(jax.nn.gelu(upward, approximate=False))
    downward = low_back(jnp.dot(active, w_down, precision=highest))
    return norm_rows(downward + b_down + hidden, gain_two, shift_two)

def reference(tokens, w_qkv, b_query, b_value, w_out, b_out, gain_one, shift_one, w_up, b_up, w_down, b_down, gain_two, shift_two, out_grad):
    float_weights = tuple((p.astype(jnp.float32) for p in (w_qkv, b_query, b_value, w_out, b_out, gain_one, shift_one, w_up, b_up, w_down, b_down, gain_two, shift_two)))
    block_rows = tokens.shape[0] // N_DP
    token_blocks = tokens.astype(jnp.float32).reshape(N_DP, block_rows, D)
    grad_blocks = out_grad.astype(jnp.float32).reshape(N_DP, block_rows, D)

    def scan_step(running, block_pair):
        block_in, block_grad = block_pair
        layer_val, pullback = jax.vjp(block_forward, block_in, *float_weights)
        gradients = pullback(block_grad)
        running = tuple((a + b for a, b in zip(running, gradients[1:])))
        return (running, (layer_val.astype(jnp.bfloat16), gradients[0]))
    empty_sums = tuple((jnp.zeros_like(p) for p in float_weights))
    running, (layer_blocks, input_blocks) = lax.scan(scan_step, empty_sums, (token_blocks, grad_blocks))
    layer_out = layer_blocks.reshape(tokens.shape[0], D)
    grad_tokens = input_blocks.reshape(tokens.shape[0], D)
    return (layer_out, grad_tokens, running[0], running[1], running[2], running[3], running[4], running[5], running[6], running[7], running[8], running[9], running[10], running[11], running[12])
```

```python
import jax
import jax.numpy as jnp
from jax import lax
from jax.sharding import PartitionSpec as P

HEAD_DIM = 64
LEN = 512


EPSILON = 1e-12
BF = jnp.bfloat16
F32 = jnp.float32


def norm_rows(resid, gain, shift):
    center = jnp.mean(resid, axis=-1, keepdims=True)
    centred = resid - center
    variance = jnp.mean(centred * centred, axis=-1, keepdims=True)
    return centred * lax.rsqrt(variance + EPSILON) * gain + shift


def gelu_exact(upward):
    return jax.nn.gelu(upward, approximate=False)


def contract_rows(left, right):
    return lax.dot_general(
        left, right, (((0,), (0,)), ((), ())), preferred_element_type=jnp.float32
    )


def times_transposed(left, right):
    return lax.dot_general(
        left, right, (((1,), (1,)), ((), ())), preferred_element_type=jnp.float32
    )


def project_qkv(gathered, qkv_flat, b_query, b_value, heads_here):
    row_total = gathered.shape[0]
    seq_count = row_total // LEN
    projected = jnp.dot(gathered, qkv_flat, preferred_element_type=jnp.float32)
    projected = projected.reshape(row_total, 3, heads_here, HEAD_DIM)
    queries = (projected[:, 0] + b_query.reshape(heads_here, HEAD_DIM)).astype(jnp.bfloat16)
    key_rows = projected[:, 1].astype(jnp.bfloat16)
    values = (projected[:, 2] + b_value.reshape(heads_here, HEAD_DIM)).astype(jnp.bfloat16)
    new_shape = (seq_count, LEN, heads_here, HEAD_DIM)
    return (queries.reshape(new_shape), key_rows.reshape(new_shape), values.reshape(new_shape))


def attend(bundle):
    seq_query, seq_keys, seq_values = bundle
    scores = jnp.einsum(
        "qhd,khd->hqk", seq_query, seq_keys, preferred_element_type=jnp.float32
    ) * HEAD_DIM ** (-0.5)
    row_peak = jnp.max(scores, axis=-1, keepdims=True)
    exponent = jnp.exp(scores - row_peak)
    denom_sum = jnp.sum(exponent, axis=-1, keepdims=True)
    prob_rows = (exponent / denom_sum).astype(jnp.bfloat16)
    context = jnp.einsum("hqk,khd->qhd", prob_rows, seq_values, preferred_element_type=jnp.float32)
    return (context.astype(jnp.bfloat16), (row_peak + jnp.log(denom_sum))[..., 0])


def attend_back(bundle):
    seq_query, seq_keys, seq_values, seq_dcontext, seq_lognorm = bundle
    score_scale = HEAD_DIM ** (-0.5)
    scores = (
        jnp.einsum("qhd,khd->hqk", seq_query, seq_keys, preferred_element_type=jnp.float32)
        * score_scale
    )
    prob_rows = jnp.exp(scores - seq_lognorm[..., None])
    d_values = jnp.einsum(
        "hqk,qhd->khd",
        prob_rows.astype(jnp.bfloat16),
        seq_dcontext,
        preferred_element_type=jnp.float32,
    )
    d_probs = jnp.einsum(
        "qhd,khd->hqk", seq_dcontext, seq_values, preferred_element_type=jnp.float32
    )
    d_scores = prob_rows * (d_probs - jnp.sum(prob_rows * d_probs, axis=-1, keepdims=True))
    d_scores = d_scores.astype(jnp.bfloat16)
    d_queries = (
        jnp.einsum("hqk,khd->qhd", d_scores, seq_keys, preferred_element_type=jnp.float32)
        * score_scale
    )
    d_keys = (
        jnp.einsum("hqk,qhd->khd", d_scores, seq_query, preferred_element_type=jnp.float32)
        * score_scale
    )
    return jnp.stack([d_queries, d_keys, d_values], axis=1)


def general_body(
    tokens,
    w_qkv,
    b_query,
    b_value,
    w_out,
    b_out,
    gain_one,
    shift_one,
    w_up,
    b_up,
    w_down,
    b_down,
    gain_two,
    shift_two,
    out_grad,
):
    own_rows, width = tokens.shape
    local_width = w_out.shape[0]
    heads_here = local_width // HEAD_DIM
    qkv_flat = w_qkv.reshape(width, 3 * local_width)
    gathered = lax.all_gather(tokens, "tensor", axis=0, tiled=True)
    row_total = gathered.shape[0]
    seq_count = row_total // LEN
    queries, key_rows, values = project_qkv(gathered, qkv_flat, b_query, b_value, heads_here)
    context, lognorm = lax.map(attend, (queries, key_rows, values))
    context = context.reshape(row_total, local_width)
    out_whole = lax.all_gather(w_out, "tensor", axis=0, tiled=True)
    own_context = lax.all_to_all(context, "tensor", split_axis=0, concat_axis=1, tiled=True)
    attended = jnp.dot(own_context, out_whole, preferred_element_type=jnp.float32)
    resid_one = attended + b_out + tokens.astype(jnp.float32)
    hidden, pull_one = jax.vjp(norm_rows, resid_one, gain_one, shift_one)
    hidden_low = hidden.astype(jnp.bfloat16)
    spread = lax.all_gather(hidden_low, "tensor", axis=0, tiled=True)
    upward = jnp.dot(spread, w_up, preferred_element_type=jnp.float32) + b_up
    active = gelu_exact(upward).astype(jnp.bfloat16)
    row_block = active
    downward = lax.psum_scatter(
        jnp.dot(row_block, w_down, preferred_element_type=jnp.float32).astype(jnp.bfloat16),
        "tensor",
        scatter_dimension=0,
        tiled=True,
    ).astype(jnp.float32)
    resid_two = downward + b_down + hidden
    result, pull_two = jax.vjp(norm_rows, resid_two, gain_two, shift_two)
    layer_out = result.astype(jnp.bfloat16)
    d_resid_two, grad_gain_two, grad_shift_two = pull_two(out_grad.astype(jnp.float32))
    grad_b_down = jnp.sum(d_resid_two, axis=0)
    ffn_rows = lax.all_gather(d_resid_two.astype(jnp.bfloat16), "tensor", axis=0, tiled=True)
    grad_w_down = contract_rows(active, ffn_rows)
    d_active = times_transposed(ffn_rows, w_down)
    gelu_pull = jax.vjp(gelu_exact, upward)[1]
    d_upward = gelu_pull(d_active)[0]
    grad_b_up = jnp.sum(d_upward, axis=0)
    d_up_low = d_upward.astype(jnp.bfloat16)
    grad_w_up = contract_rows(spread, d_up_low)
    row_block = d_up_low
    d_hidden = d_resid_two + lax.psum_scatter(
        times_transposed(row_block, w_up), "tensor", scatter_dimension=0, tiled=True
    )
    d_resid_one, grad_gain_one, grad_shift_one = pull_one(d_hidden)
    grad_b_out = jnp.sum(d_resid_one, axis=0)
    attn_rows = lax.all_gather(d_resid_one.astype(jnp.bfloat16), "tensor", axis=0, tiled=True)
    grad_w_out = contract_rows(context, attn_rows)
    d_context = times_transposed(attn_rows, w_out).astype(jnp.bfloat16)
    d_context = d_context.reshape(seq_count, LEN, heads_here, HEAD_DIM)
    d_projected = lax.map(attend_back, (queries, key_rows, values, d_context, lognorm))
    d_projected = d_projected.reshape(row_total, 3, local_width)
    grad_b_query = jnp.sum(d_projected[:, 0], axis=0)
    grad_b_value = jnp.sum(d_projected[:, 2], axis=0)
    d_proj_low = d_projected.reshape(row_total, 3 * local_width).astype(jnp.bfloat16)
    grad_w_qkv = contract_rows(gathered, d_proj_low).reshape(width, 3, local_width)
    row_block = d_proj_low
    grad_tokens = d_resid_one + lax.psum_scatter(
        times_transposed(row_block, qkv_flat).astype(jnp.bfloat16),
        "tensor",
        scatter_dimension=0,
        tiled=True,
    ).astype(jnp.float32)
    grad_w_qkv, grad_b_query, grad_b_value, grad_w_out, grad_w_up, grad_b_up, grad_w_down = (
        lax.psum(grad_w_qkv.astype(jnp.bfloat16), "dp").astype(jnp.float32),
        lax.psum(grad_b_query.astype(jnp.bfloat16), "dp").astype(jnp.float32),
        lax.psum(grad_b_value.astype(jnp.bfloat16), "dp").astype(jnp.float32),
        lax.psum(grad_w_out.astype(jnp.bfloat16), "dp").astype(jnp.float32),
        lax.psum(grad_w_up.astype(jnp.bfloat16), "dp").astype(jnp.float32),
        lax.psum(grad_b_up.astype(jnp.bfloat16), "dp").astype(jnp.float32),
        lax.psum(grad_w_down.astype(jnp.bfloat16), "dp").astype(jnp.float32),
    )
    grad_gain_one, grad_shift_one, grad_gain_two, grad_shift_two, grad_b_out, grad_b_down = (
        lax.psum(
            (grad_gain_one, grad_shift_one, grad_gain_two, grad_shift_two, grad_b_out, grad_b_down),
            ("dp", "tensor"),
        )
    )
    return (
        layer_out,
        grad_tokens,
        grad_w_qkv,
        grad_b_query,
        grad_b_value,
        grad_w_out,
        grad_b_out,
        grad_gain_one,
        grad_shift_one,
        grad_w_up,
        grad_b_up,
        grad_w_down,
        grad_b_down,
        grad_gain_two,
        grad_shift_two,
    )


def mm(left, right):
    return jnp.dot(left, right, preferred_element_type=F32)


def pair_swap(x):
    return lax.ppermute(x, "tensor", [(0, 1), (1, 0)])


class DpSum:
    def __init__(self, size):
        self.size = size
        self.index = lax.axis_index("dp")
        self.depth = size.bit_length() - 1

    def bit(self, k):
        return (self.index >> k) & 1

    def swap(self, x, k):
        return lax.ppermute(x, "dp", [(i, i ^ (1 << k)) for i in range(self.size)])

    def split(self, x, k, axis=0):
        half = x.shape[axis] // 2
        bit = self.bit(k)
        keep = lax.dynamic_slice_in_dim(x, bit * half, half, axis)
        send = lax.dynamic_slice_in_dim(x, (1 - bit) * half, half, axis)
        return keep, send

    def add(self, a, b):
        return (a.astype(F32) + b.astype(F32)).astype(BF)

    def scatter(self, x, k):
        keep, send = self.split(x, k)
        return self.add(keep, self.swap(send, k))

    def join(self, own, other, k, dtype=None):
        first = self.bit(k) == 0
        low = jnp.where(first, own, other)
        high = jnp.where(first, other, own)
        out = jnp.concatenate([low, high], axis=0)
        return out if dtype is None else out.astype(dtype)

    def gather(self, x, k, dtype=None):
        return self.join(x, self.swap(x, k), k, dtype)

    def chain(self, x, order):
        for k in order:
            x = self.scatter(x, k)
        for k in range(3, self.depth):
            x = self.add(x, self.swap(x, k))
        for k in reversed(order):
            x = self.gather(x, k)
        return x

    def weight(self, make):
        core = self.bit(0)
        other = make(1 - core).astype(BF)
        own = (make(core) + self.swap(other, 0).astype(F32)).astype(BF)
        half = own.shape[0] // 2
        parts = [self.chain(own[:half], (1, 2)), self.chain(own[half:], (2, 1))]
        return self.gather(jnp.concatenate(parts, axis=0), 0, F32)

    def everywhere(self, x):
        for k in range(self.depth):
            x = x + self.swap(x, k)
        return x


def column_half(x, which):
    half = x.shape[1] // 2
    return lax.dynamic_slice_in_dim(x, which * half, half, 1)


def pair_body(dp_size):
    def body(
        tokens,
        w_qkv,
        b_query,
        b_value,
        w_out,
        b_out,
        gain_one,
        shift_one,
        w_up,
        b_up,
        w_down,
        b_down,
        gain_two,
        shift_two,
        out_grad,
    ):
        dp = DpSum(dp_size)
        own_rows, width = tokens.shape
        local_width = w_out.shape[0]
        heads = local_width // HEAD_DIM
        hidden_width = w_up.shape[1]

        def by_head(x):
            return x.reshape(x.shape[0], heads, HEAD_DIM)

        def project(rows):
            q = (mm(rows, w_qkv[:, 0]) + b_query).astype(BF)
            k = mm(rows, w_qkv[:, 1]).astype(BF)
            v = (mm(rows, w_qkv[:, 2]) + b_value).astype(BF)
            return q, k, v

        tokens_p = pair_swap(tokens)
        q_o, k_o, v_o = project(tokens)
        q_p, k_p, v_p = project(tokens_p)
        keys = by_head(jnp.concatenate([k_o, k_p], axis=0))
        values = by_head(jnp.concatenate([v_o, v_p], axis=0))
        ctx_p, norm_p = attend((by_head(q_p), keys, values))
        ctx_p = ctx_p.reshape(own_rows, local_width)
        out_p = pair_swap(mm(ctx_p, w_out).astype(BF))
        ctx_o, norm_o = attend((by_head(q_o), keys, values))
        ctx_o = ctx_o.reshape(own_rows, local_width)
        attended = mm(ctx_o, w_out) + out_p.astype(F32)
        resid_one = attended + b_out + tokens.astype(F32)
        hidden, pull_one = jax.vjp(norm_rows, resid_one, gain_one, shift_one)
        hidden_o = hidden.astype(BF)
        hidden_p = pair_swap(hidden_o)

        def forward(rows):
            upward = mm(rows, w_up) + b_up
            active, pull = jax.vjp(gelu_exact, upward)
            slope = pull(jnp.ones_like(upward))[0]
            return active.astype(BF), slope.astype(F32)

        active_o, slope_o = forward(hidden_o)
        active_p, slope_p = forward(hidden_p)
        down_p = pair_swap(mm(active_p, w_down).astype(BF))
        downward = mm(active_o, w_down) + down_p.astype(F32)
        resid_two = downward + b_down + hidden
        result, pull_two = jax.vjp(norm_rows, resid_two, gain_two, shift_two)
        layer_out = result.astype(BF)
        d_resid_two, grad_gain_two, grad_shift_two = pull_two(out_grad.astype(F32))
        grad_b_down = jnp.sum(d_resid_two, axis=0)
        d2_o = d_resid_two.astype(BF)
        d2_p = pair_swap(d2_o)
        dup_o = times_transposed(d2_o, w_down) * slope_o
        dup_p = times_transposed(d2_p, w_down) * slope_p
        grad_b_up = jnp.sum(dup_o, axis=0) + jnp.sum(dup_p, axis=0)
        dup_o = dup_o.astype(BF)
        dup_p = dup_p.astype(BF)
        dhid_p = pair_swap(times_transposed(dup_p, w_up).astype(BF))
        d_hidden = d_resid_two + times_transposed(dup_o, w_up) + dhid_p.astype(F32)
        active = jnp.concatenate([active_o, active_p], axis=0)
        d2 = jnp.concatenate([d2_o, d2_p], axis=0)
        dup = jnp.concatenate([dup_o, dup_p], axis=0)
        spread = jnp.concatenate([hidden_o, hidden_p], axis=0)
        grad_w_down = dp.weight(lambda h: contract_rows(column_half(active, h), d2))
        grad_w_up = dp.weight(lambda h: contract_rows(column_half(spread, h), dup))

        d_resid_one, grad_gain_one, grad_shift_one = pull_one(d_hidden)
        grad_b_out = jnp.sum(d_resid_one, axis=0)
        d1_o = d_resid_one.astype(BF)
        d1_p = pair_swap(d1_o)
        d1 = jnp.concatenate([d1_o, d1_p], axis=0)
        context = jnp.concatenate([ctx_o, ctx_p], axis=0)
        grad_w_out = dp.weight(lambda h: contract_rows(column_half(context, h), d1))
        d_context = times_transposed(d1, w_out).astype(BF)
        queries = by_head(jnp.concatenate([q_o, q_p], axis=0))
        lognorm = jnp.concatenate([norm_o, norm_p], axis=1)
        d_proj = attend_back((queries, keys, values, by_head(d_context), lognorm))
        d_proj = d_proj.reshape(2 * own_rows, 3, local_width)
        grad_b_query = jnp.sum(d_proj[:, 0], axis=0)
        grad_b_value = jnp.sum(d_proj[:, 2], axis=0)
        d_low = d_proj.astype(BF)
        gathered = jnp.concatenate([tokens, tokens_p], axis=0)
        d_flat = d_low.reshape(2 * own_rows, 3 * local_width)
        grad_w_qkv = dp.weight(lambda h: contract_rows(column_half(gathered, h), d_flat))
        grad_w_qkv = grad_w_qkv.reshape(width, 3, local_width)

        def to_tokens(rows):
            return sum(times_transposed(rows[:, p], w_qkv[:, p]) for p in range(3))

        gtok_p = pair_swap(to_tokens(d_low[own_rows:]).astype(BF))
        grad_tokens = d_resid_one + to_tokens(d_low[:own_rows]) + gtok_p.astype(F32)

        both = jnp.concatenate(
            [grad_gain_one, grad_shift_one, grad_gain_two, grad_shift_two, grad_b_out, grad_b_down]
        )
        both = both + pair_swap(both)
        small = dp.everywhere(jnp.concatenate([both, grad_b_query, grad_b_value, grad_b_up]))
        sizes = [width] * 6 + [local_width, local_width, hidden_width]
        cuts = [sum(sizes[:i]) for i in range(1, len(sizes))]
        (
            grad_gain_one,
            grad_shift_one,
            grad_gain_two,
            grad_shift_two,
            grad_b_out,
            grad_b_down,
            grad_b_query,
            grad_b_value,
            grad_b_up,
        ) = jnp.split(small, cuts)
        return (
            layer_out,
            grad_tokens,
            grad_w_qkv,
            grad_b_query,
            grad_b_value,
            grad_w_out,
            grad_b_out,
            grad_gain_one,
            grad_shift_one,
            grad_w_up,
            grad_b_up,
            grad_w_down,
            grad_b_down,
            grad_gain_two,
            grad_shift_two,
        )

    return body


def solution(mesh):
    dp_size = mesh.shape["dp"]
    paired = mesh.shape["tensor"] == 2 and dp_size >= 8 and dp_size & (dp_size - 1) == 0
    pair = pair_body(dp_size)

    def body(*args):
        if paired and 2 * args[0].shape[0] == LEN:
            return pair(*args)
        return general_body(*args)

    placed = (
        P(("dp", "tensor"), None),
        P(None, None, "tensor"),
        P("tensor"),
        P("tensor"),
        P("tensor", None),
        P(),
        P(),
        P(),
        P(None, "tensor"),
        P("tensor"),
        P("tensor", None),
        P(),
        P(),
        P(),
        P(("dp", "tensor"), None),
    )
    return jax.shard_map(
        body,
        mesh=mesh,
        in_specs=placed,
        out_specs=(
            P(("dp", "tensor"), None),
            P(("dp", "tensor"), None),
            P(None, None, "tensor"),
            P("tensor"),
            P("tensor"),
            P("tensor", None),
            P(),
            P(),
            P(),
            P(None, "tensor"),
            P("tensor"),
            P("tensor", None),
            P(),
            P(),
            P(),
        ),
        check_vma=False,
    )
```

```python
import jax
import jax.numpy as jnp
from jax import lax
from jax.experimental import pallas as pl
from jax.experimental.pallas import tpu as pltpu
from jax.sharding import PartitionSpec as P

HEAD_DIM = 64
LEN = 512


EPSILON = 1e-12
BF = jnp.bfloat16
F32 = jnp.float32


def norm_rows(resid, gain, shift):
    center = jnp.mean(resid, axis=-1, keepdims=True)
    centred = resid - center
    variance = jnp.mean(centred * centred, axis=-1, keepdims=True)
    return centred * lax.rsqrt(variance + EPSILON) * gain + shift


def gelu_exact(upward):
    return jax.nn.gelu(upward, approximate=False)


def contract_rows(left, right):
    return lax.dot_general(
        left, right, (((0,), (0,)), ((), ())), preferred_element_type=jnp.float32
    )


def times_transposed(left, right):
    return lax.dot_general(
        left, right, (((1,), (1,)), ((), ())), preferred_element_type=jnp.float32
    )


def project_qkv(gathered, qkv_flat, b_query, b_value, heads_here):
    row_total = gathered.shape[0]
    seq_count = row_total // LEN
    projected = jnp.dot(gathered, qkv_flat, preferred_element_type=jnp.float32)
    projected = projected.reshape(row_total, 3, heads_here, HEAD_DIM)
    queries = (projected[:, 0] + b_query.reshape(heads_here, HEAD_DIM)).astype(jnp.bfloat16)
    key_rows = projected[:, 1].astype(jnp.bfloat16)
    values = (projected[:, 2] + b_value.reshape(heads_here, HEAD_DIM)).astype(jnp.bfloat16)
    new_shape = (seq_count, LEN, heads_here, HEAD_DIM)
    return (queries.reshape(new_shape), key_rows.reshape(new_shape), values.reshape(new_shape))


def attend(bundle):
    seq_query, seq_keys, seq_values = bundle
    scores = jnp.einsum(
        "qhd,khd->hqk", seq_query, seq_keys, preferred_element_type=jnp.float32
    ) * HEAD_DIM ** (-0.5)
    row_peak = jnp.max(scores, axis=-1, keepdims=True)
    exponent = jnp.exp(scores - row_peak)
    denom_sum = jnp.sum(exponent, axis=-1, keepdims=True)
    prob_rows = (exponent / denom_sum).astype(jnp.bfloat16)
    context = jnp.einsum("hqk,khd->qhd", prob_rows, seq_values, preferred_element_type=jnp.float32)
    return (context.astype(jnp.bfloat16), (row_peak + jnp.log(denom_sum))[..., 0])


def attend_back(bundle):
    seq_query, seq_keys, seq_values, seq_dcontext, seq_lognorm = bundle
    score_scale = HEAD_DIM ** (-0.5)
    scores = (
        jnp.einsum("qhd,khd->hqk", seq_query, seq_keys, preferred_element_type=jnp.float32)
        * score_scale
    )
    prob_rows = jnp.exp(scores - seq_lognorm[..., None])
    d_values = jnp.einsum(
        "hqk,qhd->khd",
        prob_rows.astype(jnp.bfloat16),
        seq_dcontext,
        preferred_element_type=jnp.float32,
    )
    d_probs = jnp.einsum(
        "qhd,khd->hqk", seq_dcontext, seq_values, preferred_element_type=jnp.float32
    )
    d_scores = prob_rows * (d_probs - jnp.sum(prob_rows * d_probs, axis=-1, keepdims=True))
    d_scores = d_scores.astype(jnp.bfloat16)
    d_queries = (
        jnp.einsum("hqk,khd->qhd", d_scores, seq_keys, preferred_element_type=jnp.float32)
        * score_scale
    )
    d_keys = (
        jnp.einsum("hqk,qhd->khd", d_scores, seq_query, preferred_element_type=jnp.float32)
        * score_scale
    )
    return jnp.stack([d_queries, d_keys, d_values], axis=1)


def general_body(
    tokens,
    w_qkv,
    b_query,
    b_value,
    w_out,
    b_out,
    gain_one,
    shift_one,
    w_up,
    b_up,
    w_down,
    b_down,
    gain_two,
    shift_two,
    out_grad,
):
    own_rows, width = tokens.shape
    local_width = w_out.shape[0]
    heads_here = local_width // HEAD_DIM
    qkv_flat = w_qkv.reshape(width, 3 * local_width)
    gathered = lax.all_gather(tokens, "tensor", axis=0, tiled=True)
    row_total = gathered.shape[0]
    seq_count = row_total // LEN
    queries, key_rows, values = project_qkv(gathered, qkv_flat, b_query, b_value, heads_here)
    context, lognorm = lax.map(attend, (queries, key_rows, values))
    context = context.reshape(row_total, local_width)
    out_whole = lax.all_gather(w_out, "tensor", axis=0, tiled=True)
    own_context = lax.all_to_all(context, "tensor", split_axis=0, concat_axis=1, tiled=True)
    attended = jnp.dot(own_context, out_whole, preferred_element_type=jnp.float32)
    resid_one = attended + b_out + tokens.astype(jnp.float32)
    hidden, pull_one = jax.vjp(norm_rows, resid_one, gain_one, shift_one)
    hidden_low = hidden.astype(jnp.bfloat16)
    spread = lax.all_gather(hidden_low, "tensor", axis=0, tiled=True)
    upward = jnp.dot(spread, w_up, preferred_element_type=jnp.float32) + b_up
    active = gelu_exact(upward).astype(jnp.bfloat16)
    row_block = active
    downward = lax.psum_scatter(
        jnp.dot(row_block, w_down, preferred_element_type=jnp.float32).astype(jnp.bfloat16),
        "tensor",
        scatter_dimension=0,
        tiled=True,
    ).astype(jnp.float32)
    resid_two = downward + b_down + hidden
    result, pull_two = jax.vjp(norm_rows, resid_two, gain_two, shift_two)
    layer_out = result.astype(jnp.bfloat16)
    d_resid_two, grad_gain_two, grad_shift_two = pull_two(out_grad.astype(jnp.float32))
    grad_b_down = jnp.sum(d_resid_two, axis=0)
    ffn_rows = lax.all_gather(d_resid_two.astype(jnp.bfloat16), "tensor", axis=0, tiled=True)
    grad_w_down = contract_rows(active, ffn_rows)
    d_active = times_transposed(ffn_rows, w_down)
    gelu_pull = jax.vjp(gelu_exact, upward)[1]
    d_upward = gelu_pull(d_active)[0]
    grad_b_up = jnp.sum(d_upward, axis=0)
    d_up_low = d_upward.astype(jnp.bfloat16)
    grad_w_up = contract_rows(spread, d_up_low)
    row_block = d_up_low
    d_hidden = d_resid_two + lax.psum_scatter(
        times_transposed(row_block, w_up), "tensor", scatter_dimension=0, tiled=True
    )
    d_resid_one, grad_gain_one, grad_shift_one = pull_one(d_hidden)
    grad_b_out = jnp.sum(d_resid_one, axis=0)
    attn_rows = lax.all_gather(d_resid_one.astype(jnp.bfloat16), "tensor", axis=0, tiled=True)
    grad_w_out = contract_rows(context, attn_rows)
    d_context = times_transposed(attn_rows, w_out).astype(jnp.bfloat16)
    d_context = d_context.reshape(seq_count, LEN, heads_here, HEAD_DIM)
    d_projected = lax.map(attend_back, (queries, key_rows, values, d_context, lognorm))
    d_projected = d_projected.reshape(row_total, 3, local_width)
    grad_b_query = jnp.sum(d_projected[:, 0], axis=0)
    grad_b_value = jnp.sum(d_projected[:, 2], axis=0)
    d_proj_low = d_projected.reshape(row_total, 3 * local_width).astype(jnp.bfloat16)
    grad_w_qkv = contract_rows(gathered, d_proj_low).reshape(width, 3, local_width)
    row_block = d_proj_low
    grad_tokens = d_resid_one + lax.psum_scatter(
        times_transposed(row_block, qkv_flat).astype(jnp.bfloat16),
        "tensor",
        scatter_dimension=0,
        tiled=True,
    ).astype(jnp.float32)
    grad_w_qkv, grad_b_query, grad_b_value, grad_w_out, grad_w_up, grad_b_up, grad_w_down = (
        lax.psum(grad_w_qkv.astype(jnp.bfloat16), "dp").astype(jnp.float32),
        lax.psum(grad_b_query.astype(jnp.bfloat16), "dp").astype(jnp.float32),
        lax.psum(grad_b_value.astype(jnp.bfloat16), "dp").astype(jnp.float32),
        lax.psum(grad_w_out.astype(jnp.bfloat16), "dp").astype(jnp.float32),
        lax.psum(grad_w_up.astype(jnp.bfloat16), "dp").astype(jnp.float32),
        lax.psum(grad_b_up.astype(jnp.bfloat16), "dp").astype(jnp.float32),
        lax.psum(grad_w_down.astype(jnp.bfloat16), "dp").astype(jnp.float32),
    )
    grad_gain_one, grad_shift_one, grad_gain_two, grad_shift_two, grad_b_out, grad_b_down = (
        lax.psum(
            (grad_gain_one, grad_shift_one, grad_gain_two, grad_shift_two, grad_b_out, grad_b_down),
            ("dp", "tensor"),
        )
    )
    return (
        layer_out,
        grad_tokens,
        grad_w_qkv,
        grad_b_query,
        grad_b_value,
        grad_w_out,
        grad_b_out,
        grad_gain_one,
        grad_shift_one,
        grad_w_up,
        grad_b_up,
        grad_w_down,
        grad_b_down,
        grad_gain_two,
        grad_shift_two,
    )


ANY = pl.BlockSpec(memory_space=pl.ANY)
VMEM_BYTES = 18 << 20


def mm(left, right):
    return jnp.dot(left, right, preferred_element_type=F32)


class Chain:
    def __init__(self):
        self.last = None
        self.count = 0
        self.arrivals = []

    def swap(self, x, axis, pairs):
        got = lax.ppermute(x, axis, pairs)
        self.arrivals.append((got, self.count))
        return got

    def pause(self):
        self.call(lambda: None, "pause", [], [], work=10**12)

    def call(self, kernel, name, ins, outs, grid=(1,), scalars=None, scratch=(), work=4 * 10**10):
        arrays = [x for x, _, _ in ins]
        if any(x is got and count == self.count for x in arrays for got, count in self.arrivals):
            self.pause()
        self.count += 1
        specs = [pl.BlockSpec(block, index) for _, block, index in ins]
        n_in = len(arrays)
        extra = [] if self.last is None else [self.last]
        lead = 0 if scalars is None else 1

        mark = (like((8, 128), F32), (8, 128), lambda *_: (0, 0))
        n_out = len(outs)

        def run(*refs):
            head, rest = refs[:lead], refs[lead:]
            taken, rest = rest[:n_in], rest[n_in + len(extra) :]
            rest[n_out][...] = jnp.zeros((8, 128), F32)
            kernel(*head, *taken, *rest[:n_out], *rest[n_out + 1 :])

        *result, self.last = pl.pallas_call(
            run,
            grid_spec=pltpu.PrefetchScalarGridSpec(
                num_scalar_prefetch=lead,
                grid=grid,
                in_specs=specs + [ANY] * len(extra),
                out_specs=[pl.BlockSpec(block, index) for _, block, index in list(outs) + [mark]],
                scratch_shapes=list(scratch),
            ),
            out_shape=[shape for shape, _, _ in list(outs) + [mark]],
            compiler_params=pltpu.CompilerParams(vmem_limit_bytes=VMEM_BYTES),
            cost_estimate=pl.CostEstimate(flops=work, bytes_accessed=10**6, transcendentals=0),
            name=name,
        )(*([] if scalars is None else [scalars]), *arrays, *extra)
        return result


def like(shape, dtype):
    return jax.ShapeDtypeStruct(shape, dtype)


def in_hbm(x):
    return pltpu.with_memory_space_constraint(x, pltpu.HBM)


def whole(x):
    zeros = (0,) * len(x.shape)
    return (x, x.shape, lambda *_: zeros)


def rows_of(x, count):
    return (x, (x.shape[0] // count,) + x.shape[1:], lambda i, *_: (i,) + (0,) * (len(x.shape) - 1))


def columns_of(x, width):
    return (x, (x.shape[0], width), lambda i, *_: (0, i))


def project(chain, rows, w_parts, bias):
    parts, depth, width = w_parts.shape

    def kernel(x, w, b, out):
        out[0] = (mm(x[...], w[0]) + b[0]).astype(BF)

    part = lambda i: (i, 0, 0)
    return chain.call(
        kernel,
        "project",
        [whole(rows), (w_parts, (1, depth, width), part), (bias, (1, 1, width), part)],
        [(like((parts, rows.shape[0], width), BF), (1, rows.shape[0], width), part)],
        grid=(parts,),
    )[0]


PAIR = 2 * HEAD_DIM


def pick_head(shape):
    return lax.broadcasted_iota(jnp.int32, shape, 1) < HEAD_DIM


def attention(chain, mine, first, second, w_out, out_dtype):
    _, rows, width = mine.shape
    depth = w_out.shape[1]
    steps = width // PAIR
    scale = HEAD_DIM ** (-0.5)

    def kernel(q, k_a, k_b, v_a, v_b, w, ctx, out, total):
        step = pl.program_id(0)
        low = pick_head((rows, PAIR))
        keys = jnp.concatenate([k_a[0], k_b[0]], axis=0)
        values = jnp.concatenate([v_a[0], v_b[0]], axis=0)
        found = []
        for take in (low, jnp.logical_not(low)):
            query = jnp.where(take, q[0].astype(F32), 0.0).astype(BF)
            scores = times_transposed(query, keys) * scale
            raised = jnp.exp(scores - jnp.max(scores, axis=-1, keepdims=True))
            share = raised * (1.0 / jnp.sum(raised, axis=-1, keepdims=True))
            found.append(mm(share.astype(BF), values))
        context = jnp.where(low, found[0], found[1]).astype(BF)
        ctx[...] = context
        term = mm(context, w[...])

        @pl.when(step == 0)
        def _():
            total[...] = term

        @pl.when(step > 0)
        def _():
            total[...] += term

        @pl.when(step == steps - 1)
        def _():
            out[...] = total[...].astype(out_dtype)

    def part(p):
        return lambda i: (p, 0, i)

    block = (1, rows, PAIR)
    return chain.call(
        kernel,
        "attention",
        [
            (mine, block, part(0)),
            (first, block, part(1)),
            (second, block, part(1)),
            (first, block, part(2)),
            (second, block, part(2)),
            (w_out, (PAIR, depth), lambda i: (i, 0)),
        ],
        [
            (like((rows, width), BF), (rows, PAIR), lambda i: (0, i)),
            whole(like((rows, depth), out_dtype)),
        ],
        grid=(steps,),
        scratch=[pltpu.VMEM((rows, depth), F32)],
    )


def centre(resid):
    centred = resid - jnp.mean(resid, axis=-1, keepdims=True)
    spread = lax.rsqrt(jnp.mean(centred * centred, axis=-1, keepdims=True) + EPSILON)
    return centred * spread, spread


def norm_back(unit, spread, grad):
    shared = jnp.mean(grad, axis=-1, keepdims=True)
    along = jnp.mean(grad * unit, axis=-1, keepdims=True)
    return spread * (grad - shared - unit * along)


def three_sums(sums, step, *terms):
    found = jnp.concatenate([jnp.sum(t, axis=0, keepdims=True) for t in terms], axis=0)

    @pl.when(step == 0)
    def _():
        sums[...] = found

    @pl.when(step > 0)
    def _():
        sums[...] += found


def first_norm(chain, attended, got, tokens, bias, gain, shift):
    rows, width = tokens.shape

    def kernel(a, g, t, b, gain_, shift_, resid, hidden, low):
        value = a[...] + g[...].astype(F32) + b[...] + t[...].astype(F32)
        resid[...] = value
        unit, _ = centre(value)
        out = unit * gain_[...] + shift_[...]
        hidden[...] = out
        low[...] = out.astype(BF)

    full, half = like((rows, width), F32), like((rows, width), BF)
    n = 2
    return chain.call(
        kernel,
        "first_norm",
        [rows_of(attended, n), rows_of(got, n), rows_of(tokens, n), whole(bias), whole(gain), whole(shift)],
        [rows_of(full, n), rows_of(full, n), rows_of(half, n)],
        grid=(n,),
    )


def up_and_down(chain, rows, w_up, b_up, w_down, out_dtype):
    count, width = rows.shape
    hidden = w_up.shape[1]
    block = 512
    steps = hidden // block

    def kernel(x, up, b, down, active, slope, out, total):
        step = pl.program_id(0)
        u = mm(x[...], up[...]) + b[...]
        below = 0.5 * (1.0 + lax.erf(u * (0.5**0.5)))
        act = (u * below).astype(BF)
        active[...] = act
        slope[...] = (below + u * (jnp.exp(-0.5 * u * u) * (0.5 / jnp.pi) ** 0.5)).astype(BF)
        term = mm(act, down[...])

        @pl.when(step == 0)
        def _():
            total[...] = term

        @pl.when(step > 0)
        def _():
            total[...] += term

        @pl.when(step == steps - 1)
        def _():
            out[...] = total[...].astype(out_dtype)

    return chain.call(
        kernel,
        "up_and_down",
        [
            whole(rows),
            columns_of(w_up, block),
            columns_of(b_up, block),
            (w_down, (block, width), lambda i: (i, 0)),
        ],
        [
            columns_of(like((count, hidden), BF), block),
            columns_of(like((count, hidden), BF), block),
            whole(like((count, width), out_dtype)),
        ],
        grid=(steps,),
        scratch=[pltpu.VMEM((count, width), F32)],
    )


def second_norm(chain, downward, got, bias, hidden, gain, shift, out_grad):
    rows, width = hidden.shape

    def kernel(d, g, b, h, gain_, shift_, og, layer, d_resid, d_low, sums):
        unit, spread = centre(d[...] + g[...].astype(F32) + b[...] + h[...])
        layer[...] = (unit * gain_[...] + shift_[...]).astype(BF)
        grad = og[...].astype(F32)
        back = norm_back(unit, spread, grad * gain_[...])
        d_resid[...] = back
        d_low[...] = back.astype(BF)
        three_sums(sums, pl.program_id(0), grad * unit, grad, back)

    full, half = like((rows, width), F32), like((rows, width), BF)
    n = 2
    return chain.call(
        kernel,
        "second_norm",
        [rows_of(downward, n), rows_of(got, n), whole(bias), rows_of(hidden, n), whole(gain), whole(shift), rows_of(out_grad, n)],
        [rows_of(half, n), rows_of(full, n), rows_of(half, n), whole(like((3, width), F32))],
        grid=(n,),
    )


def down_and_up_back(chain, d_rows, slope, w_down, w_up, out_dtype):
    count, width = d_rows.shape
    hidden = slope.shape[1]
    block = 512
    steps = hidden // block

    def kernel(d, s, down, up, d_up, sums, out, total):
        step = pl.program_id(0)
        grad = times_transposed(d[...], down[...]) * s[...].astype(F32)
        sums[...] = jnp.sum(grad, axis=0, keepdims=True)
        low = grad.astype(BF)
        d_up[...] = low
        term = times_transposed(low, up[...])

        @pl.when(step == 0)
        def _():
            total[...] = term

        @pl.when(step > 0)
        def _():
            total[...] += term

        @pl.when(step == steps - 1)
        def _():
            out[...] = total[...].astype(out_dtype)

    return chain.call(
        kernel,
        "down_and_up_back",
        [
            whole(d_rows),
            columns_of(slope, block),
            (w_down, (block, width), lambda i: (i, 0)),
            columns_of(w_up, block),
        ],
        [
            columns_of(like((count, hidden), BF), block),
            columns_of(like((1, hidden), F32), block),
            whole(like((count, width), out_dtype)),
        ],
        grid=(steps,),
        scratch=[pltpu.VMEM((count, width), F32)],
    )


def first_norm_back(chain, d_resid, own, got, resid, gain):
    rows, width = resid.shape

    def kernel(d, o, g, r, gain_, out, low, sums):
        unit, spread = centre(r[...])
        grad = d[...] + o[...] + g[...].astype(F32)
        back = norm_back(unit, spread, grad * gain_[...])
        out[...] = back
        low[...] = back.astype(BF)
        three_sums(sums, pl.program_id(0), grad * unit, grad, back)

    full, half = like((rows, width), F32), like((rows, width), BF)
    n = 2
    return chain.call(
        kernel,
        "first_norm_back",
        [rows_of(d_resid, n), rows_of(own, n), rows_of(got, n), rows_of(resid, n), whole(gain)],
        [rows_of(full, n), rows_of(half, n), whole(like((3, width), F32))],
        grid=(n,),
    )


def attention_back(chain, first, second, d_first, d_second, w_out):
    _, rows, width = first.shape
    depth = w_out.shape[1]
    scale = HEAD_DIM ** (-0.5)

    def kernel(qa, qb, ka, kb, va, vb, da, db, w, out_a, out_b, sums):
        keys = jnp.concatenate([ka[0], kb[0]], axis=0)
        values = jnp.concatenate([va[0], vb[0]], axis=0)
        low = pick_head((rows, PAIR))
        both_low = pick_head((2 * rows, PAIR))
        d_query, d_keys, d_values = [], [], []
        for q, d in ((qa, da), (qb, db)):
            d_context = times_transposed(d[...], w[...]).astype(BF)
            query = q[0]
            terms = []
            for take in (low, jnp.logical_not(low)):
                some = jnp.where(take, query.astype(F32), 0.0).astype(BF)
                scores = times_transposed(keys, some) * scale
                raised = jnp.exp(scores - jnp.max(scores, axis=0, keepdims=True))
                share = raised * (1.0 / jnp.sum(raised, axis=0, keepdims=True))
                d_some = jnp.where(take, d_context.astype(F32), 0.0).astype(BF)
                d_share = times_transposed(values, d_some)
                inner = jnp.sum(share * d_share, axis=0, keepdims=True)
                d_scores = (share * (d_share - inner)).astype(BF)
                terms.append(
                    (
                        contract_rows(d_scores, keys),
                        mm(d_scores, query),
                        mm(share.astype(BF), d_context),
                    )
                )
            d_query.append(jnp.where(low, terms[0][0], terms[1][0]) * scale)
            d_keys.append(jnp.where(both_low, terms[0][1], terms[1][1]) * scale)
            d_values.append(jnp.where(both_low, terms[0][2], terms[1][2]))
        key_grad = d_keys[0] + d_keys[1]
        value_grad = d_values[0] + d_values[1]
        for out, query_grad, cut in ((out_a, d_query[0], 0), (out_b, d_query[1], rows)):
            out[0] = query_grad.astype(BF)
            out[1] = key_grad[cut : cut + rows].astype(BF)
            out[2] = value_grad[cut : cut + rows].astype(BF)
        query_sum = jnp.sum(d_query[0] + d_query[1], axis=0, keepdims=True)
        sums[...] = jnp.concatenate([query_sum, jnp.sum(value_grad, axis=0, keepdims=True)], axis=0)

    def part(p):
        return lambda i: (p, 0, i)

    block = (1, rows, PAIR)
    out = (like((3, rows, width), BF), (3, rows, PAIR), lambda i: (0, 0, i))
    return chain.call(
        kernel,
        "attention_back",
        [(x, block, part(p)) for p in range(3) for x in (first, second)]
        + [whole(d_first), whole(d_second), (w_out, (PAIR, depth), lambda i: (i, 0))],
        [out, out, (like((2, width), F32), (2, PAIR), lambda i: (0, i))],
        grid=(width // PAIR,),
    )


def to_tokens(chain, d_parts, w_parts, out_dtype, adds=()):
    parts, rows, width = d_parts.shape
    depth = w_parts.shape[1]

    def kernel(d, w, *refs):
        out, total = refs[-2:]
        step = pl.program_id(0)
        term = times_transposed(d[0], w[0])

        @pl.when(step == 0)
        def _():
            total[...] = term

        @pl.when(step > 0)
        def _():
            total[...] += term

        @pl.when(step == parts - 1)
        def _():
            value = total[...]
            for ref in refs[:-2]:
                value = value + ref[...].astype(F32)
            out[...] = value.astype(out_dtype)

    part = lambda i: (i, 0, 0)
    return chain.call(
        kernel,
        "to_tokens",
        [(d_parts, (1, rows, width), part), (w_parts, (1, depth, width), part)]
        + [whole(x) for x in adds],
        [whole(like((rows, depth), out_dtype))],
        grid=(parts,),
        scratch=[pltpu.VMEM((rows, depth), F32)],
    )[0]


class Dp:
    SIZE = 16

    def __init__(self, chain):
        self.chain = chain
        self.index = lax.axis_index("dp").astype(jnp.int32)

    def bit(self, k):
        return (self.index >> k) & 1

    def swap(self, x, k):
        return self.chain.swap(x, "dp", [(i, i ^ (1 << k)) for i in range(self.SIZE)])

    def hop(self, x, got, rows):
        def kernel(a, b, out):
            out[...] = a[...]
            out[:rows, :] += b[:rows, :]

        return self.chain.call(kernel, "hop", [whole(x), whole(got)], [whole(x)])[0]


class WeightSum:
    ORDERS = ((1, 2), (2, 1))

    def __init__(self, dp, ins, product, groups, rows, columns, step):
        self.dp, self.ins, self.product, self.step = dp, ins, product, step
        self.groups, self.rows, self.columns = groups, rows, columns
        self.orders = self.ORDERS

    def multiply(self, core, got, name):
        dp, rows, groups, columns, step = self.dp, self.rows, self.groups, self.columns, self.step
        product, n_in = self.product, len(self.ins)
        n = len(self.orders)
        count = 2 * n
        bits = [dp.bit(order[0]) for order in self.orders]
        place = [2 * i + 1 - bit for i, bit in enumerate(bits)]
        place += [2 * i + bit for i, bit in enumerate(bits)]
        per_group = columns // step

        def kernel(places, *refs):
            left, rest, total = refs[:n_in], refs[n_in:-1], refs[-1]
            product(left, total)
            if got is None:
                rest[0][0] = total[...].astype(BF)
                return
            for i in range(count):
                at = pl.ds(pl.multiple_of(places[1 + i] * rows, rows), rows)
                rest[1 + i][0] = (total[at, :] + rest[0][0, at, :].astype(F32)).astype(BF)

        def along(height):
            return (1, height, step), lambda s, places: (s // per_group, 0, s % per_group)

        ins = list(self.ins)
        all_rows = like((groups, count * rows, columns), BF)
        if got is None:
            outs = [(all_rows, *along(count * rows))]
        else:
            ins.append((got, *along(count * rows)))
            outs = [(like((groups, rows, columns), BF), *along(rows))] * count
        return dp.chain.call(
            kernel,
            name,
            ins,
            outs,
            grid=(groups * per_group,),
            scalars=jnp.stack([core] + place).astype(jnp.int32),
            scratch=[pltpu.VMEM((count * rows, step), F32)],
        )

    def begin(self):
        other = self.multiply(1 - self.dp.bit(0), None, "other_core_rows")[0]
        self.other_in = self.dp.swap(other, 0)

    def own(self):
        pieces = self.multiply(self.dp.bit(0), self.other_in, "own_core_rows")
        n = len(self.orders)
        self.send, self.keep = pieces[:n], pieces[n:]

    def start(self, level):
        self.got = [self.dp.swap(x, order[level]) for x, order in zip(self.send, self.orders)]

    def halve(self):
        groups, rows, columns, n = self.groups, self.rows, self.columns, len(self.orders)
        half = rows // 2
        bits = [self.dp.bit(order[1]) for order in self.orders]
        block = (groups, half, columns)

        def kernel(places, *refs):
            p = pl.program_id(0)
            for i in range(n):
                value = (refs[i][...].astype(F32) + refs[n + i][...].astype(F32)).astype(BF)
                for step in range(2):

                    @pl.when(p == step)
                    def _():
                        refs[2 * n + n * step + i][...] = value

        def half_of(i):
            return lambda p, places: (0, jnp.where(p == 0, 1 - places[i], places[i]), 0)

        ins = [(x, block, half_of(i)) for i, x in enumerate(self.keep)]
        ins += [(x, block, half_of(i)) for i, x in enumerate(self.got)]
        outs = [whole(like(block, BF))] * (2 * n)
        pieces = self.dp.chain.call(
            kernel, "halve", ins, outs, grid=(2,), scalars=jnp.stack(bits).astype(jnp.int32)
        )
        self.send, self.keep = pieces[:n], pieces[n:]
        self.start(1)

    def middle(self):
        groups, columns, n = self.groups, self.columns, len(self.orders)
        half = self.rows // 2

        def kernel(*refs):
            for i in range(n):
                value = refs[i][...].astype(F32) + refs[n + i][...].astype(F32)
                refs[2 * n][:, i * half : (i + 1) * half, :] = value.astype(BF)

        ins = [whole(x) for x in list(self.keep) + list(self.got)]
        outs = [whole(like((groups, n * half, columns), BF))]
        self.held = self.dp.chain.call(kernel, "middle", ins, outs)[0]

    def cross(self):
        self.crossed = self.dp.swap(self.held, 3)

    def back(self):
        groups, columns, n = self.groups, self.columns, len(self.orders)
        half = self.rows // 2

        def kernel(a, b, *outs):
            for i in range(n):
                cut = slice(i * half, (i + 1) * half)
                outs[i][...] = (a[:, cut, :].astype(F32) + b[:, cut, :].astype(F32)).astype(BF)

        outs = [whole(like((groups, half, columns), BF))] * n
        self.held = self.dp.chain.call(
            kernel, "back", [whole(self.held), whole(self.crossed)], outs
        )
        self.got = [self.dp.swap(x, order[1]) for x, order in zip(self.held, self.orders)]

    def home(self):
        groups, columns, n = self.groups, self.columns, len(self.orders)
        half = self.rows // 2
        bits = [self.dp.bit(order[1]) for order in self.orders]

        def kernel(places, *refs):
            for i in range(n):
                at = pl.multiple_of(places[i] * half, half)
                other = pl.multiple_of((1 - places[i]) * half, half)
                out, all_out = refs[2 * n + i], refs[3 * n]
                start = i * 2 * half
                for source, place in ((refs[i], at), (refs[n + i], other)):
                    value = source[...]
                    out[:, pl.ds(place, half), :] = value
                    all_out[:, pl.ds(pl.multiple_of(start + place, half), half), :] = value

        ins = [whole(x) for x in list(self.held) + list(self.got)]
        outs = [whole(like((groups, 2 * half, columns), BF))] * n
        outs.append(whole(like((groups, 2 * n * half, columns), BF)))
        *self.held, self.all_held = self.dp.chain.call(
            kernel, "home", ins, outs, scalars=jnp.stack(bits).astype(jnp.int32)
        )
        self.got = [self.dp.swap(x, order[0]) for x, order in zip(self.held, self.orders)]
        self.all_in = self.dp.swap(self.all_held, 0)

    def result(self, shapes, split):
        dp, n, groups, columns, rows = self.dp, len(self.orders), self.groups, self.columns, self.rows
        got_in = [dp.swap(x, 0) for x in self.got]
        core = dp.bit(0)
        places = []
        sources = [(self.all_held, 0, core), (self.all_in, 0, 1 - core)]
        sources += [(got, 1, core) for got in self.got] + [(got, 1, 1 - core) for got in got_in]
        bits = [dp.bit(order[0]) for order in self.orders]
        for which in (core, 1 - core):
            places += [which * 2 * n + 2 * i + bit for i, bit in enumerate(bits)]
        for which in (core, 1 - core):
            places += [which * 2 * n + 2 * i + 1 - bit for i, bit in enumerate(bits)]
        arrays = [self.all_held, self.all_in] + list(self.got) + got_in
        owners = [i for i in range(2) for _ in range(n)] + list(range(2, 2 + 2 * n))
        count = len(owners)
        block = (groups, rows, columns)

        def kernel(places_ref, *refs):
            step = pl.program_id(0)
            outs = refs[len(arrays) :]
            for i in range(len(arrays)):
                first, last = owners.index(i), count - 1 - owners[::-1].index(i)

                @pl.when(jnp.logical_and(step >= first, step <= last))
                def _():
                    for out, found in zip(outs, split(refs[i])):
                        out[...] = found.astype(F32)

        def piece_map(i):
            first = owners.index(i)
            size = owners.count(i)
            return lambda p, places_ref: (0, jnp.clip(p - first, 0, size - 1), 0)

        return dp.chain.call(
            kernel,
            "assemble",
            [(x, block, piece_map(i)) for i, x in enumerate(arrays)],
            shapes,
            grid=(count,),
            scalars=jnp.stack(places).astype(jnp.int32),
        )


def pair_body(
    tokens,
    w_qkv,
    b_query,
    b_value,
    w_out,
    b_out,
    gain_one,
    shift_one,
    w_up,
    b_up,
    w_down,
    b_down,
    gain_two,
    shift_two,
    out_grad,
):
    chain = Chain()
    dp = Dp(chain)

    def pair_swap(x):
        return chain.swap(x, "tensor", [(0, 1), (1, 0)])

    own_rows, width = tokens.shape
    local_width = w_out.shape[0]
    hidden_width = w_up.shape[1]
    w_parts = in_hbm(jnp.transpose(w_qkv, (1, 0, 2)))
    w_out, w_up, w_down = in_hbm(w_out), in_hbm(w_up), in_hbm(w_down)
    bias = jnp.stack([b_query, jnp.zeros_like(b_query), b_value])[:, None, :]
    b_out, gain_one, shift_one, b_up, b_down, gain_two, shift_two = (
        x[None, :] for x in (b_out, gain_one, shift_one, b_up, b_down, gain_two, shift_two)
    )

    tokens_p = pair_swap(tokens)
    qkv_o = project(chain, tokens, w_parts, bias)
    qkv_p = project(chain, tokens_p, w_parts, bias)
    ctx_p, out_send = attention(chain, qkv_p, qkv_o, qkv_p, w_out, BF)
    out_got = pair_swap(out_send)
    ctx_o, out_own = attention(chain, qkv_o, qkv_o, qkv_p, w_out, F32)
    resid_one, hidden, hidden_o = first_norm(
        chain, out_own, out_got, tokens, b_out, gain_one, shift_one
    )
    hidden_p = pair_swap(hidden_o)
    active_o, slope_o, down_own = up_and_down(chain, hidden_o, w_up, b_up, w_down, F32)
    active_p, slope_p, down_send = up_and_down(chain, hidden_p, w_up, b_up, w_down, BF)
    down_got = pair_swap(down_send)
    layer_out, d_two, d_two_o, sums_two = second_norm(
        chain, down_own, down_got, b_down, hidden, gain_two, shift_two, out_grad
    )
    d_two_p = pair_swap(d_two_o)
    d_up_o, b_up_o, dhid_own = down_and_up_back(chain, d_two_o, slope_o, w_down, w_up, F32)

    def core_half(x):
        return (x, (own_rows, x.shape[1] // 2), lambda s, places: (0, places[0]))

    def columns_at(x, step):
        return (x, (own_rows, step), lambda s, places: (0, s))

    def plain_product(refs, total):
        total[...] = contract_rows(refs[0][...], refs[2][...])
        total[...] += contract_rows(refs[1][...], refs[3][...])

    def plain_sum(left, right, step):
        ins = [core_half(x) for x in left] + [columns_at(x, step) for x in right]
        rows, columns = left[0].shape[1], right[0].shape[1]
        return WeightSum(dp, ins, plain_product, 1, rows // 8, columns, step)

    def plain_result(total, rows, columns):
        piece = rows // 8
        shape = pltpu.HBM((1, rows, columns), F32)
        block = (1, piece, columns)
        return total.result(
            [(shape, block, lambda p, places: (0, places[p], 0))], lambda ref: (ref[...],)
        )[0][0]

    sum_down = plain_sum((active_o, active_p), (d_two_o, d_two_p), 256)
    sum_down.begin()
    d_up_p, b_up_p, dhid_send = down_and_up_back(chain, d_two_p, slope_p, w_down, w_up, BF)
    dhid_got = pair_swap(dhid_send)
    sum_down.own()
    sum_down.start(0)
    sum_up = plain_sum((hidden_o, hidden_p), (d_up_o, d_up_p), 512)
    sum_up.begin()
    d_one, d_one_o, sums_one = first_norm_back(
        chain, d_two, dhid_own, dhid_got, resid_one, gain_one
    )
    d_one_p = pair_swap(d_one_o)
    sum_down.halve()
    sum_up.own()
    sum_up.start(0)
    sum_down.middle()
    sum_down.cross()
    d_qkv_o, d_qkv_p, sums_qv = attention_back(chain, qkv_o, qkv_p, d_one_o, d_one_p, w_out)
    sum_up.halve()

    def rest_product(refs, total):
        step = pl.program_id(0)

        @pl.when(step < 3)
        def _():
            total[...] = contract_rows(refs[0][...], refs[4][0])
            total[...] += contract_rows(refs[1][...], refs[5][0])

        @pl.when(step == 3)
        def _():
            rows = local_width // 2
            for i in range(2):
                at = slice(i * rows, (i + 1) * rows)
                cut = slice(i * local_width, (i + 1) * local_width)
                total[at, :] = contract_rows(refs[2][...], refs[6][:, cut])
                total[at, :] += contract_rows(refs[3][...], refs[7][:, cut])

    def part_at(x):
        return (x, (1,) + x.shape[1:], lambda s, places: (jnp.minimum(s, 2), 0, 0))

    sum_rest = WeightSum(
        dp,
        [core_half(tokens), core_half(tokens_p), core_half(ctx_o), core_half(ctx_p)]
        + [part_at(d_qkv_o), part_at(d_qkv_p), whole(d_one_o), whole(d_one_p)],
        rest_product,
        4,
        width // 8,
        local_width,
        local_width,
    )
    sum_rest.begin()
    shared = jnp.concatenate([sums_two, sums_one], axis=0).reshape(-1)
    small = jnp.concatenate([shared, sums_qv.reshape(-1), (b_up_o + b_up_p).reshape(-1)])
    small = small.reshape(-1, 128)
    sum_up.middle()
    sum_rest.own()
    sum_rest.start(0)
    sum_down.back()
    sum_up.cross()
    sum_down.home()
    sum_rest.halve()
    sum_up.back()
    sum_rest.middle()
    sum_rest.cross()
    tokens_send = to_tokens(chain, d_qkv_p, w_parts, BF)
    tokens_got = pair_swap(tokens_send)
    sum_up.home()
    grad_w_down = plain_result(sum_down, hidden_width, width)
    small_got = pair_swap(small)
    grad_tokens = to_tokens(chain, d_qkv_o, w_parts, F32, (d_one, tokens_got))
    small = dp.hop(small, small_got, shared.shape[0] // 128)
    small_got = dp.swap(small, 0)
    sum_rest.back()
    small = dp.hop(small, small_got, small.shape[0])
    small_got = dp.swap(small, 1)
    grad_w_up = plain_result(sum_up, width, hidden_width)
    small = dp.hop(small, small_got, small.shape[0])
    small_got = dp.swap(small, 2)
    sum_rest.home()
    small = dp.hop(small, small_got, small.shape[0])
    small_got = dp.swap(small, 3)
    small = dp.hop(small, small_got, small.shape[0]).reshape(-1)
    piece = width // 8
    grad_w_qkv, grad_w_out = sum_rest.result(
        [
            (
                pltpu.HBM((3, width, local_width), F32),
                (3, piece, local_width),
                lambda p, places: (0, places[p], 0),
            ),
            (
                pltpu.HBM((local_width, width), F32),
                (piece, local_width),
                lambda p, places: (places[p] // 4 * 2 + places[p] % 2, places[p] % 4 // 2),
            ),
        ],
        lambda ref: (ref[0:3], ref[3]),
    )

    sizes = [width] * 6 + [local_width, local_width, hidden_width]
    cuts = [sum(sizes[:i]) for i in range(1, len(sizes))]
    (
        grad_gain_two,
        grad_shift_two,
        grad_b_down,
        grad_gain_one,
        grad_shift_one,
        grad_b_out,
        grad_b_query,
        grad_b_value,
        grad_b_up,
    ) = jnp.split(small, cuts)
    return (
        layer_out,
        grad_tokens,
        jnp.transpose(grad_w_qkv, (1, 0, 2)),
        grad_b_query,
        grad_b_value,
        grad_w_out,
        grad_b_out,
        grad_gain_one,
        grad_shift_one,
        grad_w_up,
        grad_b_up,
        grad_w_down,
        grad_b_down,
        grad_gain_two,
        grad_shift_two,
    )


def solution(mesh):
    paired = mesh.shape["tensor"] == 2 and mesh.shape["dp"] == Dp.SIZE

    def body(*args):
        if paired and 2 * args[0].shape[0] == LEN:
            return pair_body(*args)
        return general_body(*args)

    placed = (
        P(("dp", "tensor"), None),
        P(None, None, "tensor"),
        P("tensor"),
        P("tensor"),
        P("tensor", None),
        P(),
        P(),
        P(),
        P(None, "tensor"),
        P("tensor"),
        P("tensor", None),
        P(),
        P(),
        P(),
        P(("dp", "tensor"), None),
    )
    return jax.shard_map(
        body,
        mesh=mesh,
        in_specs=placed,
        out_specs=(
            P(("dp", "tensor"), None),
            P(("dp", "tensor"), None),
            P(None, None, "tensor"),
            P("tensor"),
            P("tensor"),
            P("tensor", None),
            P(),
            P(),
            P(),
            P(None, "tensor"),
            P("tensor"),
            P("tensor", None),
            P(),
            P(),
            P(),
        ),
        check_vma=False,
    )
```

```python
import jax
import jax.numpy as jnp
from jax import lax
from jax.experimental import pallas as pl
from jax.experimental.pallas import tpu as pltpu
from jax.sharding import PartitionSpec as P

HEAD_DIM = 64
LEN = 512


EPSILON = 1e-12
BF = jnp.bfloat16
F32 = jnp.float32


def norm_rows(resid, gain, shift):
    center = jnp.mean(resid, axis=-1, keepdims=True)
    centred = resid - center
    variance = jnp.mean(centred * centred, axis=-1, keepdims=True)
    return centred * lax.rsqrt(variance + EPSILON) * gain + shift


def gelu_exact(upward):
    return jax.nn.gelu(upward, approximate=False)


def contract_rows(left, right):
    return lax.dot_general(
        left, right, (((0,), (0,)), ((), ())), preferred_element_type=jnp.float32
    )


def times_transposed(left, right):
    return lax.dot_general(
        left, right, (((1,), (1,)), ((), ())), preferred_element_type=jnp.float32
    )


def project_qkv(gathered, qkv_flat, b_query, b_value, heads_here):
    row_total = gathered.shape[0]
    seq_count = row_total // LEN
    projected = jnp.dot(gathered, qkv_flat, preferred_element_type=jnp.float32)
    projected = projected.reshape(row_total, 3, heads_here, HEAD_DIM)
    queries = (projected[:, 0] + b_query.reshape(heads_here, HEAD_DIM)).astype(jnp.bfloat16)
    key_rows = projected[:, 1].astype(jnp.bfloat16)
    values = (projected[:, 2] + b_value.reshape(heads_here, HEAD_DIM)).astype(jnp.bfloat16)
    new_shape = (seq_count, LEN, heads_here, HEAD_DIM)
    return (queries.reshape(new_shape), key_rows.reshape(new_shape), values.reshape(new_shape))


def attend(bundle):
    seq_query, seq_keys, seq_values = bundle
    scores = jnp.einsum(
        "qhd,khd->hqk", seq_query, seq_keys, preferred_element_type=jnp.float32
    ) * HEAD_DIM ** (-0.5)
    row_peak = jnp.max(scores, axis=-1, keepdims=True)
    exponent = jnp.exp(scores - row_peak)
    denom_sum = jnp.sum(exponent, axis=-1, keepdims=True)
    prob_rows = (exponent / denom_sum).astype(jnp.bfloat16)
    context = jnp.einsum("hqk,khd->qhd", prob_rows, seq_values, preferred_element_type=jnp.float32)
    return (context.astype(jnp.bfloat16), (row_peak + jnp.log(denom_sum))[..., 0])


def attend_back(bundle):
    seq_query, seq_keys, seq_values, seq_dcontext, seq_lognorm = bundle
    score_scale = HEAD_DIM ** (-0.5)
    scores = (
        jnp.einsum("qhd,khd->hqk", seq_query, seq_keys, preferred_element_type=jnp.float32)
        * score_scale
    )
    prob_rows = jnp.exp(scores - seq_lognorm[..., None])
    d_values = jnp.einsum(
        "hqk,qhd->khd",
        prob_rows.astype(jnp.bfloat16),
        seq_dcontext,
        preferred_element_type=jnp.float32,
    )
    d_probs = jnp.einsum(
        "qhd,khd->hqk", seq_dcontext, seq_values, preferred_element_type=jnp.float32
    )
    d_scores = prob_rows * (d_probs - jnp.sum(prob_rows * d_probs, axis=-1, keepdims=True))
    d_scores = d_scores.astype(jnp.bfloat16)
    d_queries = (
        jnp.einsum("hqk,khd->qhd", d_scores, seq_keys, preferred_element_type=jnp.float32)
        * score_scale
    )
    d_keys = (
        jnp.einsum("hqk,qhd->khd", d_scores, seq_query, preferred_element_type=jnp.float32)
        * score_scale
    )
    return jnp.stack([d_queries, d_keys, d_values], axis=1)


def general_body(
    tokens,
    w_qkv,
    b_query,
    b_value,
    w_out,
    b_out,
    gain_one,
    shift_one,
    w_up,
    b_up,
    w_down,
    b_down,
    gain_two,
    shift_two,
    out_grad,
):
    own_rows, width = tokens.shape
    local_width = w_out.shape[0]
    heads_here = local_width // HEAD_DIM
    qkv_flat = w_qkv.reshape(width, 3 * local_width)
    gathered = lax.all_gather(tokens, "tensor", axis=0, tiled=True)
    row_total = gathered.shape[0]
    seq_count = row_total // LEN
    queries, key_rows, values = project_qkv(gathered, qkv_flat, b_query, b_value, heads_here)
    context, lognorm = lax.map(attend, (queries, key_rows, values))
    context = context.reshape(row_total, local_width)
    out_whole = lax.all_gather(w_out, "tensor", axis=0, tiled=True)
    own_context = lax.all_to_all(context, "tensor", split_axis=0, concat_axis=1, tiled=True)
    attended = jnp.dot(own_context, out_whole, preferred_element_type=jnp.float32)
    resid_one = attended + b_out + tokens.astype(jnp.float32)
    hidden, pull_one = jax.vjp(norm_rows, resid_one, gain_one, shift_one)
    hidden_low = hidden.astype(jnp.bfloat16)
    spread = lax.all_gather(hidden_low, "tensor", axis=0, tiled=True)
    upward = jnp.dot(spread, w_up, preferred_element_type=jnp.float32) + b_up
    active = gelu_exact(upward).astype(jnp.bfloat16)
    row_block = active
    downward = lax.psum_scatter(
        jnp.dot(row_block, w_down, preferred_element_type=jnp.float32).astype(jnp.bfloat16),
        "tensor",
        scatter_dimension=0,
        tiled=True,
    ).astype(jnp.float32)
    resid_two = downward + b_down + hidden
    result, pull_two = jax.vjp(norm_rows, resid_two, gain_two, shift_two)
    layer_out = result.astype(jnp.bfloat16)
    d_resid_two, grad_gain_two, grad_shift_two = pull_two(out_grad.astype(jnp.float32))
    grad_b_down = jnp.sum(d_resid_two, axis=0)
    ffn_rows = lax.all_gather(d_resid_two.astype(jnp.bfloat16), "tensor", axis=0, tiled=True)
    grad_w_down = contract_rows(active, ffn_rows)
    d_active = times_transposed(ffn_rows, w_down)
    gelu_pull = jax.vjp(gelu_exact, upward)[1]
    d_upward = gelu_pull(d_active)[0]
    grad_b_up = jnp.sum(d_upward, axis=0)
    d_up_low = d_upward.astype(jnp.bfloat16)
    grad_w_up = contract_rows(spread, d_up_low)
    row_block = d_up_low
    d_hidden = d_resid_two + lax.psum_scatter(
        times_transposed(row_block, w_up), "tensor", scatter_dimension=0, tiled=True
    )
    d_resid_one, grad_gain_one, grad_shift_one = pull_one(d_hidden)
    grad_b_out = jnp.sum(d_resid_one, axis=0)
    attn_rows = lax.all_gather(d_resid_one.astype(jnp.bfloat16), "tensor", axis=0, tiled=True)
    grad_w_out = contract_rows(context, attn_rows)
    d_context = times_transposed(attn_rows, w_out).astype(jnp.bfloat16)
    d_context = d_context.reshape(seq_count, LEN, heads_here, HEAD_DIM)
    d_projected = lax.map(attend_back, (queries, key_rows, values, d_context, lognorm))
    d_projected = d_projected.reshape(row_total, 3, local_width)
    grad_b_query = jnp.sum(d_projected[:, 0], axis=0)
    grad_b_value = jnp.sum(d_projected[:, 2], axis=0)
    d_proj_low = d_projected.reshape(row_total, 3 * local_width).astype(jnp.bfloat16)
    grad_w_qkv = contract_rows(gathered, d_proj_low).reshape(width, 3, local_width)
    row_block = d_proj_low
    grad_tokens = d_resid_one + lax.psum_scatter(
        times_transposed(row_block, qkv_flat).astype(jnp.bfloat16),
        "tensor",
        scatter_dimension=0,
        tiled=True,
    ).astype(jnp.float32)
    grad_w_qkv, grad_b_query, grad_b_value, grad_w_out, grad_w_up, grad_b_up, grad_w_down = (
        lax.psum(grad_w_qkv.astype(jnp.bfloat16), "dp").astype(jnp.float32),
        lax.psum(grad_b_query.astype(jnp.bfloat16), "dp").astype(jnp.float32),
        lax.psum(grad_b_value.astype(jnp.bfloat16), "dp").astype(jnp.float32),
        lax.psum(grad_w_out.astype(jnp.bfloat16), "dp").astype(jnp.float32),
        lax.psum(grad_w_up.astype(jnp.bfloat16), "dp").astype(jnp.float32),
        lax.psum(grad_b_up.astype(jnp.bfloat16), "dp").astype(jnp.float32),
        lax.psum(grad_w_down.astype(jnp.bfloat16), "dp").astype(jnp.float32),
    )
    grad_gain_one, grad_shift_one, grad_gain_two, grad_shift_two, grad_b_out, grad_b_down = (
        lax.psum(
            (grad_gain_one, grad_shift_one, grad_gain_two, grad_shift_two, grad_b_out, grad_b_down),
            ("dp", "tensor"),
        )
    )
    return (
        layer_out,
        grad_tokens,
        grad_w_qkv,
        grad_b_query,
        grad_b_value,
        grad_w_out,
        grad_b_out,
        grad_gain_one,
        grad_shift_one,
        grad_w_up,
        grad_b_up,
        grad_w_down,
        grad_b_down,
        grad_gain_two,
        grad_shift_two,
    )


ANY = pl.BlockSpec(memory_space=pl.ANY)
VMEM_BYTES = 18 << 20


def mm(left, right):
    return jnp.dot(left, right, preferred_element_type=F32)


class Chain:
    def __init__(self):
        self.last = None
        self.count = 0
        self.arrivals = []

    def swap(self, x, axis, pairs):
        got = lax.ppermute(x, axis, pairs)
        self.arrivals.append((got, self.count))
        return got

    def pause(self):
        self.call(lambda: None, "pause", [], [], work=10**12)

    def call(self, kernel, name, ins, outs, grid=(1,), scalars=None, scratch=(), work=4 * 10**10):
        arrays = [x for x, _, _ in ins]
        if any(x is got and count == self.count for x in arrays for got, count in self.arrivals):
            self.pause()
        self.count += 1
        specs = [pl.BlockSpec(block, index) for _, block, index in ins]
        n_in = len(arrays)
        extra = [] if self.last is None else [self.last]
        lead = 0 if scalars is None else 1

        mark = (like((8, 128), F32), (8, 128), lambda *_: (0, 0))
        n_out = len(outs)

        def run(*refs):
            head, rest = refs[:lead], refs[lead:]
            taken, rest = rest[:n_in], rest[n_in + len(extra) :]
            rest[n_out][...] = jnp.zeros((8, 128), F32)
            kernel(*head, *taken, *rest[:n_out], *rest[n_out + 1 :])

        *result, self.last = pl.pallas_call(
            run,
            grid_spec=pltpu.PrefetchScalarGridSpec(
                num_scalar_prefetch=lead,
                grid=grid,
                in_specs=specs + [ANY] * len(extra),
                out_specs=[pl.BlockSpec(block, index) for _, block, index in list(outs) + [mark]],
                scratch_shapes=list(scratch),
            ),
            out_shape=[shape for shape, _, _ in list(outs) + [mark]],
            compiler_params=pltpu.CompilerParams(vmem_limit_bytes=VMEM_BYTES),
            cost_estimate=pl.CostEstimate(flops=work, bytes_accessed=10**6, transcendentals=0),
            name=name,
        )(*([] if scalars is None else [scalars]), *arrays, *extra)
        return result


def like(shape, dtype):
    return jax.ShapeDtypeStruct(shape, dtype)


def in_hbm(x):
    return pltpu.with_memory_space_constraint(x, pltpu.HBM)


def whole(x):
    zeros = (0,) * len(x.shape)
    return (x, x.shape, lambda *_: zeros)


def rows_of(x, count):
    return (x, (x.shape[0] // count,) + x.shape[1:], lambda i, *_: (i,) + (0,) * (len(x.shape) - 1))


def columns_of(x, width):
    return (x, (x.shape[0], width), lambda i, *_: (0, i))


def project(chain, rows, w_parts, bias):
    parts, depth, width = w_parts.shape

    def kernel(x, w, b, out):
        out[0] = (mm(x[...], w[0]) + b[0]).astype(BF)

    part = lambda i: (i, 0, 0)
    return chain.call(
        kernel,
        "project",
        [whole(rows), (w_parts, (1, depth, width), part), (bias, (1, 1, width), part)],
        [(like((parts, rows.shape[0], width), BF), (1, rows.shape[0], width), part)],
        grid=(parts,),
    )[0]


PAIR = 2 * HEAD_DIM


def pick_head(shape):
    return lax.broadcasted_iota(jnp.int32, shape, 1) < HEAD_DIM


def attention(chain, mine, first, second, w_out, out_dtype):
    _, rows, width = mine.shape
    depth = w_out.shape[1]
    steps = width // PAIR
    scale = HEAD_DIM ** (-0.5)

    def kernel(q, k_a, k_b, v_a, v_b, w, ctx, out, total):
        step = pl.program_id(0)
        low = pick_head((rows, PAIR))
        keys = jnp.concatenate([k_a[0], k_b[0]], axis=0)
        values = jnp.concatenate([v_a[0], v_b[0]], axis=0)
        found = []
        for take in (low, jnp.logical_not(low)):
            query = jnp.where(take, q[0].astype(F32), 0.0).astype(BF)
            scores = times_transposed(query, keys) * scale
            raised = jnp.exp(scores - jnp.max(scores, axis=-1, keepdims=True))
            share = raised * (1.0 / jnp.sum(raised, axis=-1, keepdims=True))
            found.append(mm(share.astype(BF), values))
        context = jnp.where(low, found[0], found[1]).astype(BF)
        ctx[...] = context
        term = mm(context, w[...])

        @pl.when(step == 0)
        def _():
            total[...] = term

        @pl.when(step > 0)
        def _():
            total[...] += term

        @pl.when(step == steps - 1)
        def _():
            out[...] = total[...].astype(out_dtype)

    def part(p):
        return lambda i: (p, 0, i)

    block = (1, rows, PAIR)
    return chain.call(
        kernel,
        "attention",
        [
            (mine, block, part(0)),
            (first, block, part(1)),
            (second, block, part(1)),
            (first, block, part(2)),
            (second, block, part(2)),
            (w_out, (PAIR, depth), lambda i: (i, 0)),
        ],
        [
            (like((rows, width), BF), (rows, PAIR), lambda i: (0, i)),
            whole(like((rows, depth), out_dtype)),
        ],
        grid=(steps,),
        scratch=[pltpu.VMEM((rows, depth), F32)],
    )


def centre(resid):
    centred = resid - jnp.mean(resid, axis=-1, keepdims=True)
    spread = lax.rsqrt(jnp.mean(centred * centred, axis=-1, keepdims=True) + EPSILON)
    return centred * spread, spread


def norm_back(unit, spread, grad):
    shared = jnp.mean(grad, axis=-1, keepdims=True)
    along = jnp.mean(grad * unit, axis=-1, keepdims=True)
    return spread * (grad - shared - unit * along)


def three_sums(sums, step, *terms):
    found = jnp.concatenate([jnp.sum(t, axis=0, keepdims=True) for t in terms], axis=0)

    @pl.when(step == 0)
    def _():
        sums[...] = found

    @pl.when(step > 0)
    def _():
        sums[...] += found


def first_norm(chain, attended, got, tokens, bias, gain, shift):
    rows, width = tokens.shape

    def kernel(a, g, t, b, gain_, shift_, resid, hidden, low):
        value = a[...] + g[...].astype(F32) + b[...] + t[...].astype(F32)
        resid[...] = value
        unit, _ = centre(value)
        out = unit * gain_[...] + shift_[...]
        hidden[...] = out
        low[...] = out.astype(BF)

    full, half = like((rows, width), F32), like((rows, width), BF)
    n = 2
    return chain.call(
        kernel,
        "first_norm",
        [rows_of(attended, n), rows_of(got, n), rows_of(tokens, n), whole(bias), whole(gain), whole(shift)],
        [rows_of(full, n), rows_of(full, n), rows_of(half, n)],
        grid=(n,),
    )


def up_and_down(chain, rows, w_up, b_up, w_down, out_dtype):
    count, width = rows.shape
    hidden = w_up.shape[1]
    block = 512
    steps = hidden // block

    def kernel(x, up, b, down, active, slope, out, total):
        step = pl.program_id(0)
        u = mm(x[...], up[...]) + b[...]
        below = 0.5 * (1.0 + lax.erf(u * (0.5**0.5)))
        act = (u * below).astype(BF)
        active[...] = act
        slope[...] = (below + u * (jnp.exp(-0.5 * u * u) * (0.5 / jnp.pi) ** 0.5)).astype(BF)
        term = mm(act, down[...])

        @pl.when(step == 0)
        def _():
            total[...] = term

        @pl.when(step > 0)
        def _():
            total[...] += term

        @pl.when(step == steps - 1)
        def _():
            out[...] = total[...].astype(out_dtype)

    return chain.call(
        kernel,
        "up_and_down",
        [
            whole(rows),
            columns_of(w_up, block),
            columns_of(b_up, block),
            (w_down, (block, width), lambda i: (i, 0)),
        ],
        [
            columns_of(like((count, hidden), BF), block),
            columns_of(like((count, hidden), BF), block),
            whole(like((count, width), out_dtype)),
        ],
        grid=(steps,),
        scratch=[pltpu.VMEM((count, width), F32)],
    )


def second_norm(chain, downward, got, bias, hidden, gain, shift, out_grad):
    rows, width = hidden.shape

    def kernel(d, g, b, h, gain_, shift_, og, layer, d_resid, d_low, sums):
        unit, spread = centre(d[...] + g[...].astype(F32) + b[...] + h[...])
        layer[...] = (unit * gain_[...] + shift_[...]).astype(BF)
        grad = og[...].astype(F32)
        back = norm_back(unit, spread, grad * gain_[...])
        d_resid[...] = back
        d_low[...] = back.astype(BF)
        three_sums(sums, pl.program_id(0), grad * unit, grad, back)

    full, half = like((rows, width), F32), like((rows, width), BF)
    n = 2
    return chain.call(
        kernel,
        "second_norm",
        [rows_of(downward, n), rows_of(got, n), whole(bias), rows_of(hidden, n), whole(gain), whole(shift), rows_of(out_grad, n)],
        [rows_of(half, n), rows_of(full, n), rows_of(half, n), whole(like((3, width), F32))],
        grid=(n,),
    )


def down_and_up_back(chain, d_rows, slope, w_down, w_up, out_dtype):
    count, width = d_rows.shape
    hidden = slope.shape[1]
    block = 512
    steps = hidden // block

    def kernel(d, s, down, up, d_up, sums, out, total):
        step = pl.program_id(0)
        grad = times_transposed(d[...], down[...]) * s[...].astype(F32)
        sums[...] = jnp.sum(grad, axis=0, keepdims=True)
        low = grad.astype(BF)
        d_up[...] = low
        term = times_transposed(low, up[...])

        @pl.when(step == 0)
        def _():
            total[...] = term

        @pl.when(step > 0)
        def _():
            total[...] += term

        @pl.when(step == steps - 1)
        def _():
            out[...] = total[...].astype(out_dtype)

    return chain.call(
        kernel,
        "down_and_up_back",
        [
            whole(d_rows),
            columns_of(slope, block),
            (w_down, (block, width), lambda i: (i, 0)),
            columns_of(w_up, block),
        ],
        [
            columns_of(like((count, hidden), BF), block),
            columns_of(like((1, hidden), F32), block),
            whole(like((count, width), out_dtype)),
        ],
        grid=(steps,),
        scratch=[pltpu.VMEM((count, width), F32)],
    )


def first_norm_back(chain, d_resid, own, got, resid, gain):
    rows, width = resid.shape

    def kernel(d, o, g, r, gain_, out, low, sums):
        unit, spread = centre(r[...])
        grad = d[...] + o[...] + g[...].astype(F32)
        back = norm_back(unit, spread, grad * gain_[...])
        out[...] = back
        low[...] = back.astype(BF)
        three_sums(sums, pl.program_id(0), grad * unit, grad, back)

    full, half = like((rows, width), F32), like((rows, width), BF)
    n = 2
    return chain.call(
        kernel,
        "first_norm_back",
        [rows_of(d_resid, n), rows_of(own, n), rows_of(got, n), rows_of(resid, n), whole(gain)],
        [rows_of(full, n), rows_of(half, n), whole(like((3, width), F32))],
        grid=(n,),
    )


def attention_back(chain, first, second, d_first, d_second, w_out, half):
    _, rows, width = first.shape
    width = width // 2
    skip = half * (width // PAIR)
    depth = w_out.shape[1]
    scale = HEAD_DIM ** (-0.5)

    def kernel(qa, qb, ka, kb, va, vb, da, db, w, out_a, out_b, sums):
        keys = jnp.concatenate([ka[0], kb[0]], axis=0)
        values = jnp.concatenate([va[0], vb[0]], axis=0)
        low = pick_head((rows, PAIR))
        both_low = pick_head((2 * rows, PAIR))
        d_query, d_keys, d_values = [], [], []
        for q, d in ((qa, da), (qb, db)):
            d_context = times_transposed(d[...], w[...]).astype(BF)
            query = q[0]
            terms = []
            for take in (low, jnp.logical_not(low)):
                some = jnp.where(take, query.astype(F32), 0.0).astype(BF)
                scores = times_transposed(keys, some) * scale
                raised = jnp.exp(scores - jnp.max(scores, axis=0, keepdims=True))
                share = raised * (1.0 / jnp.sum(raised, axis=0, keepdims=True))
                d_some = jnp.where(take, d_context.astype(F32), 0.0).astype(BF)
                d_share = times_transposed(values, d_some)
                inner = jnp.sum(share * d_share, axis=0, keepdims=True)
                d_scores = (share * (d_share - inner)).astype(BF)
                terms.append(
                    (
                        contract_rows(d_scores, keys),
                        mm(d_scores, query),
                        mm(share.astype(BF), d_context),
                    )
                )
            d_query.append(jnp.where(low, terms[0][0], terms[1][0]) * scale)
            d_keys.append(jnp.where(both_low, terms[0][1], terms[1][1]) * scale)
            d_values.append(jnp.where(both_low, terms[0][2], terms[1][2]))
        key_grad = d_keys[0] + d_keys[1]
        value_grad = d_values[0] + d_values[1]
        for out, query_grad, cut in ((out_a, d_query[0], 0), (out_b, d_query[1], rows)):
            out[0] = query_grad.astype(BF)
            out[1] = key_grad[cut : cut + rows].astype(BF)
            out[2] = value_grad[cut : cut + rows].astype(BF)
        query_sum = jnp.sum(d_query[0] + d_query[1], axis=0, keepdims=True)
        sums[...] = jnp.concatenate([query_sum, jnp.sum(value_grad, axis=0, keepdims=True)], axis=0)

    def part(p):
        return lambda i: (p, 0, i + skip)

    block = (1, rows, PAIR)
    out = (like((3, rows, width), BF), (3, rows, PAIR), lambda i: (0, 0, i))
    return chain.call(
        kernel,
        "attention_back",
        [(x, block, part(p)) for p in range(3) for x in (first, second)]
        + [whole(d_first), whole(d_second), (w_out, (PAIR, depth), lambda i: (i + skip, 0))],
        [out, out, (like((2, width), F32), (2, PAIR), lambda i: (0, i))],
        grid=(width // PAIR,),
    )


def to_tokens(chain, d_halves, w_parts, out_dtype, adds=()):
    parts, rows, width = d_halves[0].shape
    depth = w_parts.shape[1]

    def kernel(d_a, d_b, w, *refs):
        out, total = refs[-2:]
        step = pl.program_id(0)
        term = times_transposed(d_a[0], w[0, :, :width]) + times_transposed(d_b[0], w[0, :, width:])

        @pl.when(step == 0)
        def _():
            total[...] = term

        @pl.when(step > 0)
        def _():
            total[...] += term

        @pl.when(step == parts - 1)
        def _():
            value = total[...]
            for ref in refs[:-2]:
                value = value + ref[...].astype(F32)
            out[...] = value.astype(out_dtype)

    part = lambda i: (i, 0, 0)
    return chain.call(
        kernel,
        "to_tokens",
        [(d, (1, rows, width), part) for d in d_halves]
        + [(w_parts, (1, depth, 2 * width), part)]
        + [whole(x) for x in adds],
        [whole(like((rows, depth), out_dtype))],
        grid=(parts,),
        scratch=[pltpu.VMEM((rows, depth), F32)],
    )[0]


class Dp:
    SIZE = 16

    def __init__(self, chain):
        self.chain = chain
        self.index = lax.axis_index("dp").astype(jnp.int32)

    def bit(self, k):
        return (self.index >> k) & 1

    def swap(self, x, k):
        return self.chain.swap(x, "dp", [(i, i ^ (1 << k)) for i in range(self.SIZE)])

    def hop(self, x, got, rows):
        def kernel(a, b, out):
            out[...] = a[...]
            out[:rows, :] += b[:rows, :]

        return self.chain.call(kernel, "hop", [whole(x), whole(got)], [whole(x)])[0]


class WeightSum:
    ORDERS = ((1, 2), (2, 1))

    def __init__(self, dp, ins, product, groups, rows, columns, step):
        self.dp, self.ins, self.product, self.step = dp, ins, product, step
        self.groups, self.rows, self.columns = groups, rows, columns
        self.orders = self.ORDERS

    def multiply(self, core, got, name):
        dp, rows, groups, columns, step = self.dp, self.rows, self.groups, self.columns, self.step
        product, n_in = self.product, len(self.ins)
        n = len(self.orders)
        count = 2 * n
        bits = [dp.bit(order[0]) for order in self.orders]
        place = [2 * i + 1 - bit for i, bit in enumerate(bits)]
        place += [2 * i + bit for i, bit in enumerate(bits)]
        per_group = columns // step

        def kernel(places, *refs):
            left, rest, total = refs[:n_in], refs[n_in:-1], refs[-1]
            product(left, total)
            if got is None:
                rest[0][0] = total[...].astype(BF)
                return
            for i in range(count):
                at = pl.ds(pl.multiple_of(places[1 + i] * rows, rows), rows)
                rest[1 + i][0] = (total[at, :] + rest[0][0, at, :].astype(F32)).astype(BF)

        def along(height):
            return (1, height, step), lambda s, places: (s // per_group, 0, s % per_group)

        ins = list(self.ins)
        all_rows = like((groups, count * rows, columns), BF)
        if got is None:
            outs = [(all_rows, *along(count * rows))]
        else:
            ins.append((got, *along(count * rows)))
            outs = [(like((groups, rows, columns), BF), *along(rows))] * count
        return dp.chain.call(
            kernel,
            name,
            ins,
            outs,
            grid=(groups * per_group,),
            scalars=jnp.stack([core] + place).astype(jnp.int32),
            scratch=[pltpu.VMEM((count * rows, step), F32)],
        )

    def begin(self):
        other = self.multiply(1 - self.dp.bit(0), None, "other_core_rows")[0]
        self.other_in = self.dp.swap(other, 0)

    def own(self):
        pieces = self.multiply(self.dp.bit(0), self.other_in, "own_core_rows")
        n = len(self.orders)
        self.send, self.keep = pieces[:n], pieces[n:]

    def start(self, level):
        self.got = [self.dp.swap(x, order[level]) for x, order in zip(self.send, self.orders)]

    def halve(self):
        groups, rows, columns, n = self.groups, self.rows, self.columns, len(self.orders)
        half = rows // 2
        bits = [self.dp.bit(order[1]) for order in self.orders]
        block = (groups, half, columns)

        def kernel(places, *refs):
            p = pl.program_id(0)
            for i in range(n):
                value = (refs[i][...].astype(F32) + refs[n + i][...].astype(F32)).astype(BF)
                for step in range(2):

                    @pl.when(p == step)
                    def _():
                        refs[2 * n + n * step + i][...] = value

        def half_of(i):
            return lambda p, places: (0, jnp.where(p == 0, 1 - places[i], places[i]), 0)

        ins = [(x, block, half_of(i)) for i, x in enumerate(self.keep)]
        ins += [(x, block, half_of(i)) for i, x in enumerate(self.got)]
        outs = [whole(like(block, BF))] * (2 * n)
        pieces = self.dp.chain.call(
            kernel, "halve", ins, outs, grid=(2,), scalars=jnp.stack(bits).astype(jnp.int32)
        )
        self.send, self.keep = pieces[:n], pieces[n:]
        self.start(1)

    def middle(self):
        groups, columns, n = self.groups, self.columns, len(self.orders)
        half = self.rows // 2

        def kernel(*refs):
            for i in range(n):
                value = refs[i][...].astype(F32) + refs[n + i][...].astype(F32)
                refs[2 * n][:, i * half : (i + 1) * half, :] = value.astype(BF)

        ins = [whole(x) for x in list(self.keep) + list(self.got)]
        outs = [whole(like((groups, n * half, columns), BF))]
        self.held = self.dp.chain.call(kernel, "middle", ins, outs)[0]

    def cross(self):
        self.crossed = self.dp.swap(self.held, 3)

    def back(self):
        groups, columns, n = self.groups, self.columns, len(self.orders)
        half = self.rows // 2

        def kernel(a, b, *outs):
            for i in range(n):
                cut = slice(i * half, (i + 1) * half)
                outs[i][...] = (a[:, cut, :].astype(F32) + b[:, cut, :].astype(F32)).astype(BF)

        outs = [whole(like((groups, half, columns), BF))] * n
        self.held = self.dp.chain.call(
            kernel, "back", [whole(self.held), whole(self.crossed)], outs
        )
        self.got = [self.dp.swap(x, order[1]) for x, order in zip(self.held, self.orders)]

    def home(self, early=False):
        groups, columns, n = self.groups, self.columns, len(self.orders)
        half = self.rows // 2
        bits = [self.dp.bit(order[1]) for order in self.orders]

        def kernel(places, *refs):
            for i in range(n):
                at = pl.multiple_of(places[i] * half, half)
                other = pl.multiple_of((1 - places[i]) * half, half)
                start = i * 2 * half
                for source, place in ((refs[i], at), (refs[n + i], other)):
                    value = source[...]
                    refs[2 * n + i][:, pl.ds(place, half), :] = value
                    if early:
                        both = pl.ds(pl.multiple_of(start + place, half), half)
                        refs[3 * n][:, both, :] = value

        ins = [whole(x) for x in list(self.held) + list(self.got)]
        outs = [whole(like((groups, 2 * half, columns), BF))] * n
        if early:
            outs.append(whole(like((groups, 2 * n * half, columns), BF)))
        found = self.dp.chain.call(
            kernel, "home", ins, outs, scalars=jnp.stack(bits).astype(jnp.int32)
        )
        self.held, self.all_held = found[:n], found[n:]
        self.got = [self.dp.swap(x, order[0]) for x, order in zip(self.held, self.orders)]

        self.all_in = [self.dp.swap(x, 0) for x in self.all_held]

    def join(self):
        groups, columns, n, rows = self.groups, self.columns, len(self.orders), self.rows
        bits = [self.dp.bit(order[0]) for order in self.orders]

        def kernel(places, *refs):
            for i in range(n):
                for source, which in ((refs[i], places[i]), (refs[n + i], 1 - places[i])):
                    at = pl.multiple_of((2 * i + which) * rows, rows)
                    refs[2 * n][:, pl.ds(at, rows), :] = source[...]

        ins = [whole(x) for x in list(self.held) + list(self.got)]
        outs = [whole(like((groups, 2 * n * rows, columns), BF))]
        self.half = self.dp.chain.call(
            kernel, "join", ins, outs, scalars=jnp.stack(bits).astype(jnp.int32)
        )[0]
        self.half_in = self.dp.swap(self.half, 0)

    def result(self, shapes, split):
        dp, n, groups, columns, rows = self.dp, len(self.orders), self.groups, self.columns, self.rows
        core = dp.bit(0)
        places = []
        if self.all_held:
            got_in = [dp.swap(x, 0) for x in self.got]
            arrays = self.all_held + self.all_in + list(self.got) + got_in
            owners = [i for i in range(2) for _ in range(n)] + list(range(2, 2 + 2 * n))
            bits = [dp.bit(order[0]) for order in self.orders]
            for which in (core, 1 - core):
                places += [which * 2 * n + 2 * i + bit for i, bit in enumerate(bits)]
            for which in (core, 1 - core):
                places += [which * 2 * n + 2 * i + 1 - bit for i, bit in enumerate(bits)]
        else:
            arrays = [self.half, self.half_in]
            owners = [i for i in range(2) for _ in range(2 * n)]
            for which in (core, 1 - core):
                places += [which * 2 * n + i for i in range(2 * n)]
        count = len(owners)
        block = (groups, rows, columns)

        def kernel(places_ref, *refs):
            step = pl.program_id(0)
            outs = refs[len(arrays) :]
            for i in range(len(arrays)):
                first, last = owners.index(i), count - 1 - owners[::-1].index(i)

                @pl.when(jnp.logical_and(step >= first, step <= last))
                def _():
                    for out, found in zip(outs, split(refs[i])):
                        out[...] = found.astype(F32)

        def piece_map(i):
            first = owners.index(i)
            size = owners.count(i)
            return lambda p, places_ref: (0, jnp.clip(p - first, 0, size - 1), 0)

        return dp.chain.call(
            kernel,
            "assemble",
            [(x, block, piece_map(i)) for i, x in enumerate(arrays)],
            shapes,
            grid=(count,),
            scalars=jnp.stack(places).astype(jnp.int32),
        )


def pair_body(
    tokens,
    w_qkv,
    b_query,
    b_value,
    w_out,
    b_out,
    gain_one,
    shift_one,
    w_up,
    b_up,
    w_down,
    b_down,
    gain_two,
    shift_two,
    out_grad,
):
    chain = Chain()
    dp = Dp(chain)

    def pair_swap(x):
        return chain.swap(x, "tensor", [(0, 1), (1, 0)])

    own_rows, width = tokens.shape
    local_width = w_out.shape[0]
    hidden_width = w_up.shape[1]
    w_parts = jnp.transpose(w_qkv, (1, 0, 2))
    w_up_back, w_down_back = in_hbm(w_up), in_hbm(w_down)
    bias = jnp.stack([b_query, jnp.zeros_like(b_query), b_value])[:, None, :]
    b_out, gain_one, shift_one, b_up, b_down, gain_two, shift_two = (
        x[None, :] for x in (b_out, gain_one, shift_one, b_up, b_down, gain_two, shift_two)
    )

    tokens_p = pair_swap(tokens)
    qkv_o = project(chain, tokens, w_parts, bias)
    qkv_p = project(chain, tokens_p, w_parts, bias)
    ctx_p, out_send = attention(chain, qkv_p, qkv_o, qkv_p, w_out, BF)
    out_got = pair_swap(out_send)
    ctx_o, out_own = attention(chain, qkv_o, qkv_o, qkv_p, w_out, F32)
    resid_one, hidden, hidden_o = first_norm(
        chain, out_own, out_got, tokens, b_out, gain_one, shift_one
    )
    hidden_p = pair_swap(hidden_o)
    active_o, slope_o, down_own = up_and_down(chain, hidden_o, w_up, b_up, w_down, F32)
    active_p, slope_p, down_send = up_and_down(chain, hidden_p, w_up, b_up, w_down, BF)
    down_got = pair_swap(down_send)
    layer_out, d_two, d_two_o, sums_two = second_norm(
        chain, down_own, down_got, b_down, hidden, gain_two, shift_two, out_grad
    )
    d_two_p = pair_swap(d_two_o)
    d_up_o, b_up_o, dhid_own = down_and_up_back(
        chain, d_two_o, slope_o, w_down_back, w_up_back, F32
    )

    def core_half(x):
        return (x, (own_rows, x.shape[1] // 2), lambda s, places: (0, places[0]))

    def columns_at(x, step):
        return (x, (own_rows, step), lambda s, places: (0, s))

    def plain_product(refs, total):
        total[...] = contract_rows(refs[0][...], refs[2][...])
        total[...] += contract_rows(refs[1][...], refs[3][...])

    def plain_sum(left, right, step):
        ins = [core_half(x) for x in left] + [columns_at(x, step) for x in right]
        rows, columns = left[0].shape[1], right[0].shape[1]
        return WeightSum(dp, ins, plain_product, 1, rows // 8, columns, step)

    def plain_result(total, rows, columns):
        piece = rows // 8
        shape = pltpu.HBM((1, rows, columns), F32)
        block = (1, piece, columns)
        return total.result(
            [(shape, block, lambda p, places: (0, places[p], 0))], lambda ref: (ref[...],)
        )[0][0]

    sum_down = plain_sum((active_o, active_p), (d_two_o, d_two_p), 256)
    sum_down.begin()
    d_up_p, b_up_p, dhid_send = down_and_up_back(
        chain, d_two_p, slope_p, w_down_back, w_up_back, BF
    )
    dhid_got = pair_swap(dhid_send)
    sum_down.own()
    sum_down.start(0)
    sum_up = plain_sum((hidden_o, hidden_p), (d_up_o, d_up_p), 512)
    sum_up.begin()
    d_one, d_one_o, sums_one = first_norm_back(
        chain, d_two, dhid_own, dhid_got, resid_one, gain_one
    )
    d_one_p = pair_swap(d_one_o)
    sum_down.halve()
    early = attention_back(chain, qkv_o, qkv_p, d_one_o, d_one_p, w_out, 0)
    sum_down.middle()
    sum_down.cross()
    sum_up.own()
    sum_up.start(0)
    late = attention_back(chain, qkv_o, qkv_p, d_one_o, d_one_p, w_out, 1)
    d_qkv_o, d_qkv_p = (early[0], late[0]), (early[1], late[1])
    sums_qv = jnp.concatenate([early[2], late[2]], axis=1)

    def rest_product(refs, total):
        step = pl.program_id(0)

        @pl.when(step < 3)
        def _():
            for i in range(2):
                cut = slice(i * local_width // 2, (i + 1) * local_width // 2)
                total[:, cut] = contract_rows(refs[0][...], refs[4 + i][0])
                total[:, cut] += contract_rows(refs[1][...], refs[6 + i][0])

        @pl.when(step == 3)
        def _():
            rows = local_width // 2
            for i in range(2):
                at = slice(i * rows, (i + 1) * rows)
                cut = slice(i * local_width, (i + 1) * local_width)
                total[at, :] = contract_rows(refs[2][...], refs[8][:, cut])
                total[at, :] += contract_rows(refs[3][...], refs[9][:, cut])

    def part_at(x):
        return (x, (1,) + x.shape[1:], lambda s, places: (jnp.minimum(s, 2), 0, 0))

    sum_rest = WeightSum(
        dp,
        [core_half(tokens), core_half(tokens_p), core_half(ctx_o), core_half(ctx_p)]
        + [part_at(x) for x in d_qkv_o + d_qkv_p]
        + [whole(d_one_o), whole(d_one_p)],
        rest_product,
        4,
        width // 8,
        local_width,
        local_width,
    )
    sum_rest.begin()
    shared = jnp.concatenate([sums_two, sums_one], axis=0).reshape(-1)
    small = jnp.concatenate([shared, sums_qv.reshape(-1), (b_up_o + b_up_p).reshape(-1)])
    small = small.reshape(-1, 128)
    sum_up.halve()
    sum_rest.own()
    sum_rest.start(0)
    sum_up.middle()
    sum_down.back()
    sum_up.cross()
    sum_rest.halve()
    sum_down.home()
    sum_up.back()
    sum_rest.middle()
    small, sum_rest.held = lax.optimization_barrier((small, sum_rest.held))
    sum_rest.cross()
    sum_up.home()
    sum_down.join()
    small_got = pair_swap(small)
    tokens_send = to_tokens(chain, d_qkv_p, w_parts, BF)
    tokens_got = pair_swap(tokens_send)
    grad_w_down = plain_result(sum_down, hidden_width, width)
    small = dp.hop(small, small_got, shared.shape[0] // 128)
    small_got = dp.swap(small, 0)
    sum_rest.back()
    sum_up.join()
    small = dp.hop(small, small_got, small.shape[0])
    small_got = dp.swap(small, 1)
    grad_tokens = to_tokens(chain, d_qkv_o, w_parts, F32, (d_one, tokens_got))
    small = dp.hop(small, small_got, small.shape[0])
    small_got = dp.swap(small, 2)
    sum_rest.home(early=True)
    small = dp.hop(small, small_got, small.shape[0])
    small_got = dp.swap(small, 3)
    grad_w_up = plain_result(sum_up, width, hidden_width)
    sum_rest.got, chain.last = lax.optimization_barrier((sum_rest.got, chain.last))
    small = dp.hop(small, small_got, small.shape[0]).reshape(-1)
    piece = width // 8
    grad_w_qkv, grad_w_out = sum_rest.result(
        [
            (
                pltpu.HBM((3, width, local_width), F32),
                (3, piece, local_width),
                lambda p, places: (0, places[p], 0),
            ),
            (
                pltpu.HBM((local_width, width), F32),
                (piece, local_width),
                lambda p, places: (places[p] // 4 * 2 + places[p] % 2, places[p] % 4 // 2),
            ),
        ],
        lambda ref: (ref[0:3], ref[3]),
    )

    sizes = [width] * 6 + [local_width, local_width, hidden_width]
    cuts = [sum(sizes[:i]) for i in range(1, len(sizes))]
    (
        grad_gain_two,
        grad_shift_two,
        grad_b_down,
        grad_gain_one,
        grad_shift_one,
        grad_b_out,
        grad_b_query,
        grad_b_value,
        grad_b_up,
    ) = jnp.split(small, cuts)
    return (
        layer_out,
        grad_tokens,
        jnp.transpose(grad_w_qkv, (1, 0, 2)),
        grad_b_query,
        grad_b_value,
        grad_w_out,
        grad_b_out,
        grad_gain_one,
        grad_shift_one,
        grad_w_up,
        grad_b_up,
        grad_w_down,
        grad_b_down,
        grad_gain_two,
        grad_shift_two,
    )


def solution(mesh):
    paired = mesh.shape["tensor"] == 2 and mesh.shape["dp"] == Dp.SIZE

    def body(*args):
        if paired and 2 * args[0].shape[0] == LEN:
            return pair_body(*args)
        return general_body(*args)

    placed = (
        P(("dp", "tensor"), None),
        P(None, None, "tensor"),
        P("tensor"),
        P("tensor"),
        P("tensor", None),
        P(),
        P(),
        P(),
        P(None, "tensor"),
        P("tensor"),
        P("tensor", None),
        P(),
        P(),
        P(),
        P(("dp", "tensor"), None),
    )
    return jax.shard_map(
        body,
        mesh=mesh,
        in_specs=placed,
        out_specs=(
            P(("dp", "tensor"), None),
            P(("dp", "tensor"), None),
            P(None, None, "tensor"),
            P("tensor"),
            P("tensor"),
            P("tensor", None),
            P(),
            P(),
            P(),
            P(None, "tensor"),
            P("tensor"),
            P("tensor", None),
            P(),
            P(),
            P(),
        ),
        check_vma=False,
    )
```
